128 devices in a mesh: dp: 16 (over z, x_hi, core), seq: 8 (over y, x_lo).
Axes of the slice: x: 4 (x_hi: 2, x_lo: 2; x = x_hi * 2 + x_lo), y: 4, z: 4, core: 2. Of those that a mesh axis runs over, the one named last changes fastest.
Arguments:
- inputs: bfloat16 [32, 1024, 576], P('dp', 'seq'), may hold values from -6 to 6
- segment_ids: int32 [32, 1024], P('dp'), may hold values from 0 to 64, as said below
- norm_attn: bfloat16 [576], P('dp'), may hold values from 0.5 to 1.5
- w_query: bfloat16 [576, 576], P('dp'), may hold values from -0.25 to 0.25
- w_key: bfloat16 [576, 192], P('dp'), may hold values from -0.25 to 0.25
- w_value: bfloat16 [576, 192], P('dp'), may hold values from -0.25 to 0.25
- w_out: bfloat16 [576, 576], P('dp'), may hold values from -1 to 1
- norm_mlp: bfloat16 [576], P('dp'), may hold values from 0.5 to 1.5
- w_gate: bfloat16 [576, 1536], P(None, ('dp', 'seq')), may hold values from -0.25 to 0.25
- w_up: bfloat16 [576, 1536], P(None, ('dp', 'seq')), may hold values from -0.25 to 0.25
- w_down: bfloat16 [1536, 576], P(('dp', 'seq')), may hold values from -0.15625 to 0.15625
- cotangent: bfloat16 [32, 1024, 576], P('dp', 'seq'), may hold values from -6 to 6
Outputs:
- output: bfloat16 [32, 1024, 576], P('dp', 'seq')
- grad_inputs: bfloat16 [32, 1024, 576], P('dp', 'seq')
- grad_norm_attn: float32 [576], P('dp')
- grad_w_query: float32 [576, 576], P('dp')
- grad_w_key: float32 [576, 192], P('dp')
- grad_w_value: float32 [576, 192], P('dp')
- grad_w_out: float32 [576, 576], P('dp')
- grad_norm_mlp: float32 [576], P('dp')
- grad_w_gate: float32 [576, 1536], P(None, ('dp', 'seq'))
- grad_w_up: float32 [576, 1536], P(None, ('dp', 'seq'))
- grad_w_down: float32 [1536, 576], P(('dp', 'seq'))
The draws below stay inside these ranges and needn't reach their ends.
Inputs may be any that keep to these rules, and one draw needn't show every extreme that they name: `segment_ids`: each row starts at 0, never falls and rises by at most one from one position to the next, and its last id is exactly 64; in every sequence one document covers positions 127 through 1024 - 128.
All inputs are finite; a program needn't handle non-finite values.
Results may differ from the reference program's by a relative error of at most 0.023.
Values may be sent and summed in bfloat16 or wider, within the bound.
A program may use at most 128 MiB of HBM per device.

```python
import jax
import jax.numpy as jnp
from jax import lax

D = 576
FF = 1536
QUERY_HEADS = 9
KV_HEADS = 3
HEAD_WIDTH = 64
SEQ_LEN = 1024
QDIM = 576
KVDIM = 192
LOCAL_LEN = 128
SEQUENCES = 32


def draw_segment_ids(key, part):
    key = jax.random.fold_in(key, 17)
    border_places = jnp.concatenate([jnp.arange(1, LOCAL_LEN, dtype=jnp.int32), jnp.arange(SEQ_LEN - LOCAL_LEN + 1, SEQ_LEN, dtype=jnp.int32)])
    border_count = 2 * (LOCAL_LEN - 1)
    row_keys = jax.random.split(key, SEQUENCES)
    orders = jax.vmap(lambda row_key: jax.random.permutation(row_key, border_count))(row_keys)
    flags = jnp.where(orders < LOCAL_LEN // 2, 1, 0).astype(jnp.int32)
    breaks = jnp.zeros((SEQUENCES, SEQ_LEN), jnp.int32).at[:, border_places].set(flags)
    return jnp.cumsum(breaks, axis=1).astype(jnp.int32)


def block_scale(key, shape, cuts, least, high):
    def one(position, parts):
        draws = jax.random.uniform(jax.random.fold_in(jax.random.fold_in(key, 6), position), (parts,), jnp.float32, least / len(cuts), high / len(cuts))
        return jnp.repeat(jnp.exp(draws), shape[position] // parts).reshape((-1,) + (1,) * (len(shape) - position - 1))

    loudness = one(*cuts[0])
    for cut in cuts[1:]:
        loudness = loudness * one(*cut)
    return loudness


def bell_draw(rng, shape, width, most, shards=(), kind=jnp.bfloat16):
    array = jax.random.normal(rng, shape, jnp.float32) * width
    if len(shards) > 0:
        array = block_scale(rng, shape, shards, -0.22, 0.18) * array
    return jnp.clip(array, min=-most, max=most).astype(kind)


def setup_inputs(seed: int = 0) -> dict:
    seeds = jax.random.split(jax.random.key(seed), 13)
    inputs = bell_draw(seeds[0], (SEQUENCES, SEQ_LEN, D), 1.0, 6.0, ((0, 16), (1, 8)))
    segment_ids = draw_segment_ids(jax.random.fold_in(seeds[12], 71), 0)
    norm_attn = jnp.clip(1.0 + 0.1 * jax.random.normal(seeds[2], (D,), jnp.float32), 0.5, 1.5).astype(jnp.bfloat16)
    w_query = bell_draw(seeds[3], (D, QDIM), D ** -0.5, 0.25, ((0, 16),))
    w_key = bell_draw(seeds[4], (D, KVDIM), D ** -0.5, 0.25, ((0, 16),))
    w_value = bell_draw(seeds[5], (D, KVDIM), D ** -0.5, 0.25, ((0, 16),))
    w_out = bell_draw(seeds[6], (QDIM, D), (QDIM // 16) ** -0.5, 1.0, ((0, 16),))
    norm_mlp = jnp.clip(1.0 + 0.1 * jax.random.normal(seeds[7], (D,), jnp.float32), 0.5, 1.5).astype(jnp.bfloat16)
    w_gate = bell_draw(seeds[8], (D, FF), D ** -0.5, 0.25, ((1, 128),))
    w_up = bell_draw(seeds[9], (D, FF), D ** -0.5, 0.25, ((1, 128),))
    w_down = bell_draw(seeds[10], (FF, D), FF ** -0.5, 0.15625, ((0, 128),))
    cotangent = bell_draw(seeds[11], (SEQUENCES, SEQ_LEN, D), 1.0, 6.0, ((0, 16), (1, 8)))
    return {"inputs": inputs, "segment_ids": segment_ids, "norm_attn": norm_attn, "w_query": w_query, "w_key": w_key, "w_value": w_value, "w_out": w_out, "norm_mlp": norm_mlp, "w_gate": w_gate, "w_up": w_up, "w_down": w_down, "cotangent": cotangent}


@jax.custom_vjp
def low(v):
    return lax.optimization_barrier(v.astype(jnp.bfloat16)).astype(jnp.float32)

@jax.custom_vjp
def low_back(v):
    return v

def low_keep(v):
    return (low(v), None)

def low_pass(kept, grad):
    return (grad,)

def back_keep(v):
    return (v, None)

def back_low(kept, grad):
    return (low(grad),)
low.defvjp(low_keep, low_pass)
low_back.defvjp(back_keep, back_low)
ROPE_BASE = 100000.0
NORM_EPS = 1e-05
MASKED = -1e+30

def matmul(left_side, right_side):
    return jnp.dot(left_side, right_side, precision=lax.Precision.HIGHEST)

def rms_norm(value_rows, gain_row):
    return value_rows * lax.rsqrt(lax.optimization_barrier(jnp.mean(value_rows * value_rows, axis=-1, keepdims=True)) + NORM_EPS) * gain_row

def token_positions(segments):
    earlier = lax.optimization_barrier(jnp.sum((segments[None, :] < segments[:, None]).astype(jnp.int32), axis=1))
    return jnp.arange(segments.shape[0], dtype=jnp.int32) - earlier

def rotary(positions):
    half_dim = HEAD_WIDTH // 2
    frequency = ROPE_BASE ** (-(2.0 * jnp.arange(half_dim, dtype=jnp.float32)) / HEAD_WIDTH)
    angles = positions.astype(jnp.float32)[:, None] * frequency[None, :]
    return (jnp.cos(angles)[:, None, :], jnp.sin(angles)[:, None, :])

def rotate(vectors, cosine_table, sine_table):
    half_dim = vectors.shape[-1] // 2
    first_half = vectors[..., :half_dim]
    second = vectors[..., half_dim:]
    return jnp.concatenate([first_half * cosine_table - second * sine_table, second * cosine_table + first_half * sine_table], axis=-1)

def layer_one(hidden, params, segments):
    gain_attn, query_w, key_w, value_w, out_w, gain_mlp, gate_w, up_w, down_w = params
    token_length = hidden.shape[0]
    group_size = QUERY_HEADS // KV_HEADS
    cosine_table, sine_table = rotary(token_positions(segments))
    normed_one = low(rms_norm(hidden, gain_attn))
    query_pre = low_back(matmul(normed_one, query_w))
    key_pre = low_back(matmul(normed_one, key_w))
    value_pre = low_back(matmul(normed_one, value_w))
    query_rows = low(rotate(query_pre.reshape(token_length, QUERY_HEADS, HEAD_WIDTH), cosine_table, sine_table))
    query_rows = query_rows.reshape(token_length, KV_HEADS, group_size, HEAD_WIDTH)
    key_rows = low(rotate(key_pre.reshape(token_length, KV_HEADS, HEAD_WIDTH), cosine_table, sine_table))
    value_rows = low(value_pre).reshape(token_length, KV_HEADS, HEAD_WIDTH)
    score_matrix = low_back(jnp.einsum('aymo,zyo->ymaz', query_rows, key_rows, precision=lax.Precision.HIGHEST) * HEAD_WIDTH ** (-0.5))
    places = jnp.arange(token_length, dtype=jnp.int32)
    allowed = (segments[:, None] == segments[None, :]) & (places[None, :] <= places[:, None])
    score_matrix = jnp.where(allowed[None, None], score_matrix, MASKED)
    attention_output = low(jax.nn.softmax(score_matrix, axis=-1))
    merged_heads = jnp.einsum('moei,imz->emoz', attention_output, value_rows, precision=lax.Precision.HIGHEST).reshape(token_length, QUERY_HEADS * HEAD_WIDTH)
    merged_heads = low(low_back(merged_heads))
    middle = hidden + low_back(matmul(merged_heads, out_w))
    normed_two = low(rms_norm(middle, gain_mlp))
    gate_value = low_back(matmul(normed_two, gate_w))
    up_value = low_back(matmul(normed_two, up_w))
    activated = low(jax.nn.silu(gate_value) * up_value)
    return middle + low_back(matmul(activated, down_w))

def reference(inputs, segment_ids, norm_attn, w_query, w_key, w_value, w_out, norm_mlp, w_gate, w_up, w_down, cotangent):
    params = tuple((weight.astype(jnp.float32) for weight in (norm_attn, w_query, w_key, w_value, w_out, norm_mlp, w_gate, w_up, w_down)))

    def forward(tokens, weights):
        per_sequence = jax.checkpoint(layer_one)

        def advance(carried, batch_item):
            return (carried, per_sequence(batch_item[0], weights, batch_item[1]))
        return lax.scan(advance, jnp.zeros((), jnp.float32), (tokens, segment_ids))[1]
    result, pullback = jax.vjp(forward, inputs.astype(jnp.float32), params)
    grad_tokens, grad_params = pullback(cotangent.astype(jnp.float32))
    grad_gain_attn, grad_query_w, grad_key_w, grad_value_w, grad_out_w, grad_gain_mlp, grad_gate_w, grad_up_w, grad_down_w = grad_params
    return (result.astype(jnp.bfloat16), grad_tokens.astype(jnp.bfloat16), grad_gain_attn, grad_query_w, grad_key_w, grad_value_w, grad_out_w, grad_gain_mlp, grad_gate_w, grad_up_w, grad_down_w)
```

```python
import functools

import jax
import jax.numpy as jnp
from jax import lax
from jax.experimental import pallas as pl
from jax.experimental.pallas import tpu as pltpu
from jax.sharding import PartitionSpec as P

MESH = pl.DeviceIdType.MESH
F32 = jnp.float32
BF16 = jnp.bfloat16

D = 576
FF = 1536
QUERY_HEADS = 9
KV_HEADS = 3
HEAD_WIDTH = 64
ROPE_BASE = 100000.0
NORM_EPS = 1e-05
MASKED = -1e30

ROWS = 36
PAD = 48
BLOCKS = 16
DP_ROWS = BLOCKS * PAD
ORDERS = (("x", "y", "z"), ("y", "z", "x"), ("z", "x", "y"))


def dot_nn(a, b):
    return lax.dot_general(a, b, (((1,), (0,)), ((), ())), preferred_element_type=F32)


def dot_nt(a, b):
    return lax.dot_general(a, b, (((1,), (1,)), ((), ())), preferred_element_type=F32)


def dot_tn(a, b):
    return lax.dot_general(a, b, (((0,), (0,)), ((), ())), preferred_element_type=F32)


def iota(shape, dim):
    return lax.broadcasted_iota(jnp.int32, shape, dim)


def one_hot(cond):
    return jnp.where(cond, 1.0, 0.0).astype(BF16)


class Place:
    def __init__(self):
        self.dp = lax.axis_index("dp")
        self.seq = lax.axis_index("seq")
        self.z = self.dp // 4
        self.x_hi = (self.dp // 2) % 2
        self.core = self.dp % 2
        self.y = self.seq // 2
        self.x_lo = self.seq % 2
        self.x = 2 * self.x_hi + self.x_lo

    def at(self, x, y, z, core):
        return (z * 4 + (x // 2) * 2 + core, y * 2 + x % 2)

    def coordinate(self, axis):
        return {"x": self.x, "y": self.y, "z": self.z}[axis]

    def ring(self, axis, step):
        here = {"x": self.x, "y": self.y, "z": self.z}
        here[axis] = (here[axis] + step + 4) % 4
        return self.at(here["x"], here["y"], here["z"], self.core)

    def other_core(self):
        return (self.dp + 1 - 2 * self.core, self.seq)

    def group(self, dz, dx):
        z = (self.z + dz + 4) % 4
        x_hi = (self.x_hi + dx) % 2
        index = z * 2 + x_hi
        return (index * 2 + self.core, self.seq), index

    def rank(self, step):
        return (self.dp, (self.seq + step + 8) % 8)


class Net:
    def __init__(self, send, recv):
        self.send, self.recv, self.used = send, recv, 0
        self.unsent = []

    def new(self):
        self.used += 1
        return self.used - 1

    def copy(self, slot, src, dst, device):
        return pltpu.make_async_remote_copy(
            src_ref=src,
            dst_ref=dst,
            send_sem=self.send.at[slot],
            recv_sem=self.recv.at[slot],
            device_id=device,
            device_id_type=MESH,
        )

    def start(self, slot, src, dst, device):
        copy = self.copy(slot, src, dst, device)
        copy.start()
        self.unsent.append(copy)

    def arrived(self, slot, dst, device):
        self.copy(slot, dst, dst, device).wait_recv()

    def finish(self):
        for copy in self.unsent:
            copy.wait_send()


GROUP_STEPS = [(dz, dx) for dz in range(4) for dx in range(2) if (dz, dx) != (0, 0)]


class Summed:
    def __init__(self, net, place, refs):
        self.net, self.place = net, place
        self.mine, self.from_core, self.chip, self.from_group, self.one, self.from_rank = refs
        self.core_slot = net.new()
        self.group_slots = [net.new() for _ in GROUP_STEPS]
        self.rank_slots = [net.new() for _ in range(7)]

    def begin(self):
        place = self.place
        self.net.start(
            self.core_slot, self.mine.at[1 - place.core], self.from_core, place.other_core()
        )

    def over_group(self):
        place, net = self.place, self.net
        net.arrived(self.core_slot, self.from_core, place.other_core())
        self.chip[...] = (
            self.mine[place.core].astype(F32) + self.from_core[...].astype(F32)
        ).astype(BF16)
        for k, (dz, dx) in enumerate(GROUP_STEPS):
            device, index = place.group(dz, dx)
            net.start(self.group_slots[k], self.chip.at[index], self.from_group.at[k], device)

    def over_ranks(self):
        place, net = self.place, self.net
        for k, (dz, dx) in enumerate(GROUP_STEPS):
            device, _ = place.group(-dz, dx)
            net.arrived(self.group_slots[k], self.from_group.at[k], device)
        total = self.chip[place.z * 2 + place.x_hi].astype(F32)
        for k in range(7):
            total += self.from_group[k].astype(F32)
        self.one[...] = total.astype(BF16)
        for k in range(7):
            net.start(self.rank_slots[k], self.one, self.from_rank.at[k], place.rank(k + 1))

    def result(self):
        place, net = self.place, self.net
        for k in range(7):
            net.arrived(self.rank_slots[k], self.from_rank.at[k], place.rank(-k - 1))
        total = self.one[...].astype(F32)
        for k in range(7):
            total += self.from_rank[k].astype(F32)
        return total


def swap_halves(tile):
    first = (iota(tile.shape, 1) & 32) == 0
    return jnp.where(first, pltpu.roll(tile, 96, 1), pltpu.roll(tile, 32, 1))


def kernel(
    x_ref, seg_ref, a1_ref, a2_ref, wg_ref, wu_ref, wd_ref, dy_ref, freq_ref,
    out_ref, gx_ref, gna_ref, gq_ref, gk_ref, gv_ref, go_ref, gnm_ref, gg_ref, gu_ref, gd_ref,
    s,
):
    place = Place()
    net = Net(s["send"], s["recv"])
    rank = place.seq

    barrier = pltpu.get_barrier_semaphore()
    peers = [place.ring(axis, step) for axis in "xyz" for step in (1, 2, 3)]
    peers += [place.other_core()]
    peers += [place.group(dz, 1)[0] for dz in (1, 2, 3)]
    flipped = place.x + 1 - 2 * place.x_lo
    peers += [place.at(flipped, (place.y + dy) % 4, place.z, place.core) for dy in (1, 2, 3)]
    for peer in peers:
        pl.semaphore_signal(barrier, inc=1, device_id=peer, device_id_type=MESH)

    row, col = iota((16, 12), 0), iota((16, 12), 1)
    down = wd_ref[...]
    for p in range(3):
        tile = jnp.zeros((16, D), F32)
        for t, ref in enumerate((wg_ref, wu_ref, wd_ref)):
            pick = one_hot(((row >> 2) == t) & (col == 4 * p + (row & 3)))
            tile += dot_nn(pick, down) if t == 2 else dot_nt(pick, ref[...])
        s["tile"][p] = tile.astype(BF16)

    pl.semaphore_wait(barrier, len(peers))

    a1, a2 = s["a1"], s["a2"]
    other_dp = place.other_core()[0]
    a_slots = {}
    for name, ref, whole in (("a1", a1_ref, a1), ("a2", a2_ref, a2)):
        group_slots = [net.new() for _ in GROUP_STEPS]
        core_slots = [net.new() for _ in range(8)]
        a_slots[name] = (group_slots, core_slots)
    ff_slots = [[[net.new() for _ in range(3)] for _ in range(3)] for _ in range(3)]
    dy_slot, n2_slot, out_slot, dn2_slot = (net.new() for _ in range(4))

    def send_own(name, ref, whole):
        group_slots, core_slots = a_slots[name]
        for k, (dz, dx) in enumerate(GROUP_STEPS):
            net.start(group_slots[k], ref, whole.at[place.dp], place.group(dz, dx)[0])
        net.start(core_slots[7], ref, whole.at[place.dp], place.other_core())
        whole[place.dp] = ref[...]

    def pass_on(name, whole):
        group_slots, core_slots = a_slots[name]
        for k, (dz, dx) in enumerate(GROUP_STEPS):
            device, index = place.group(-dz, dx)
            block = whole.at[index * 2 + place.core]
            net.arrived(group_slots[k], block, device)
            net.start(core_slots[k], block, block, place.other_core())

    def have_all(name, whole):
        group_slots, core_slots = a_slots[name]
        for k, (dz, dx) in enumerate(GROUP_STEPS):
            _, index = place.group(-dz, dx)
            net.arrived(core_slots[k], whole.at[index * 2 + 1 - place.core], place.other_core())
        net.arrived(core_slots[7], whole.at[other_dp], place.other_core())

    send_own("a1", a1_ref, a1)
    for p, (one, _, _) in enumerate(ORDERS):
        mine = place.coordinate(one)
        s["first"][p, mine] = s["tile"][p]
        for d in (1, 2, 3):
            net.start(
                ff_slots[p][0][d - 1], s["tile"].at[p], s["first"].at[p, mine], place.ring(one, d)
            )
    send_own("a2", a2_ref, a2)
    s["dy"][0] = dy_ref[...].reshape(256, D)
    net.start(dy_slot, s["dy"].at[0], s["dy"].at[1], place.other_core())

    row = iota((D, DP_ROWS), 0).astype(F32)
    col = iota((D, DP_ROWS), 1).astype(F32)
    s["spread"][...] = one_hot(col - row == 12.0 * jnp.floor((row + 0.5) * (1.0 / ROWS)))
    lane = iota((128, 128), 1)
    for b in range(2):
        own = seg_ref[pl.ds(b, 1), pl.ds(pl.multiple_of(rank * 128, 128), 128)].astype(F32)
        own = jnp.transpose(jnp.broadcast_to(own, (128, 128)))
        earlier = jnp.zeros((128, 128), F32)
        for c in range(8):
            part = seg_ref[pl.ds(b, 1), pl.ds(128 * c, 128)].astype(F32)
            earlier += jnp.where(part < own, 1.0, 0.0)
        begin = jnp.sum(earlier, axis=1, keepdims=True)
        here = (iota((128, 1), 0) + rank * 128).astype(F32)
        angle = (here - begin) * freq_ref[...]
        s["cos"][pl.ds(128 * b, 128)] = jnp.cos(angle)
        sine = jnp.sin(angle)
        s["sin"][pl.ds(128 * b, 128)] = jnp.where((lane & 32) == 0, -sine, sine)
        for k in range(8):
            key = (lane + 128 * (rank - k)).astype(F32)
            s["bias"][b, :, pl.ds(128 * k, 128)] = jnp.where(
                (key >= begin) & (key <= here), 0.0, MASKED
            )
    x = x_ref[...].reshape(256, D)
    x32 = x.astype(F32)
    inv1 = lax.rsqrt(jnp.sum(x32 * x32, axis=1, keepdims=True) * (1.0 / D) + NORM_EPS)
    s["inv1"][...] = inv1
    s["unit1"][...] = dot_nn(x, s["spread"][...]) * inv1
    for k in range(1, 8):

        @pl.when(k > rank)
        def _(k=k):
            s["kv"][k] = jnp.zeros((2, 128, 384), BF16)

    row, col = iota((PAD, 64), 0), iota((PAD, 64), 1)
    pack = one_hot(col == (((row >> 2) & 3) << 4) + ((row >> 4) << 2) + (row & 3))
    row, col = iota((64, PAD), 0), iota((64, PAD), 1)
    unpack = one_hot(row == (((col >> 2) & 3) << 4) + ((col >> 4) << 2) + (col & 3))

    def ff_second():
        for p, (one, two, three) in enumerate(ORDERS):
            mine = place.coordinate(one)
            for d in (1, 2, 3):
                net.arrived(
                    ff_slots[p][0][d - 1], s["first"].at[p, (mine + 4 - d) % 4], place.ring(one, -d)
                )
            block = s["w"].at[p, place.coordinate(three), place.coordinate(two)]
            block[...] = dot_nn(pack, s["first"][p].reshape(64, D)).astype(BF16)
            for d in (1, 2, 3):
                net.start(ff_slots[p][1][d - 1], block, block, place.ring(two, d))

    def ff_third():
        for p, (_, two, three) in enumerate(ORDERS):
            mine, last = place.coordinate(two), place.coordinate(three)
            for d in (1, 2, 3):
                net.arrived(
                    ff_slots[p][1][d - 1], s["w"].at[p, last, (mine + 4 - d) % 4], place.ring(two, -d)
                )
            block = s["w"].at[p, last]
            for d in (1, 2, 3):
                net.start(ff_slots[p][2][d - 1], block, block, place.ring(three, d))

    def ff_have(p):
        three = ORDERS[p][2]
        last = place.coordinate(three)
        for d in (1, 2, 3):
            net.arrived(
                ff_slots[p][2][d - 1], s["w"].at[p, (last + 4 - d) % 4], place.ring(three, -d)
            )

    ff_second()
    pass_on("a1", a1)
    have_all("a1", a1)

    gains = jnp.transpose(a1[:, :, pl.ds(896, 128)].reshape(DP_ROWS, 128).astype(F32))
    gain1 = gains[64:65]
    s["gain1"][...] = gain1
    gain2 = dot_nt(gains[64:80].astype(BF16), s["spread"][...])[1:2]
    s["gain2"][...] = gain2
    s["n1"][...] = (s["unit1"][...] * gain1).astype(BF16)
    pre = dot_nn(s["n1"][...], a1[...].reshape(DP_ROWS, 1024))
    cos, sin = s["cos"][...], s["sin"][...]
    lane = iota((256, 128), 1)
    for t in range(8):
        tile = pre[:, 128 * t : 128 * t + 128]
        if t != 2:
            turned = tile * cos + swap_halves(tile) * sin
            tile = jnp.where(lane < 64, turned, tile) if t == 1 else turned
        if t < 3:
            s["kv"][0, :, :, pl.ds(128 * t, 128)] = tile.astype(BF16).reshape(2, 128, 128)
        else:
            tile = (tile * HEAD_WIDTH**-0.5).astype(BF16).reshape(2, 128, 128)
            s["q"][:, :, pl.ds(128 * t - 384, 128)] = tile

    kv_slots = [net.new() for _ in range(7)]
    kv_copies = []
    for k in range(1, 8):
        copy = net.copy(kv_slots[k - 1], s["kv"].at[0], s["kv"].at[k], place.rank(k))
        kv_copies.append(copy)
        pl.when(rank + k <= 7)(copy.start)
    ff_third()
    pass_on("a2", a2)
    for k in range(1, 8):
        pl.when(k <= rank)(
            functools.partial(net.arrived, kv_slots[k - 1], s["kv"].at[k], place.rank(-k))
        )

    def heads(value, group):
        return jnp.concatenate(
            [value[:, 64 * h : 64 * h + 64] for h in range(3 * group, 3 * group + 3)], axis=0
        )

    @pl.loop(0, 2)
    def _(b):
        bias = s["bias"][b]
        for g in range(3):
            query = heads(s["q"][b], g)
            keys = s["kv"][:, b, :, pl.ds(64 * g, 64)].reshape(1024, 64)
            values = s["kv"][:, b, :, pl.ds(192 + 64 * g, 64)].reshape(1024, 64)
            score = (dot_nt(query, keys).reshape(3, 128, 1024) + bias[None]).reshape(384, 1024)
            top = jnp.max(score, axis=1, keepdims=True)
            score = jnp.exp(score - top)
            inv = 1.0 / jnp.sum(score, axis=1, keepdims=True)
            weight = score.astype(BF16)
            s["attn"][b, g] = weight
            s["inv_sum"][b, g] = inv
            mixed = (dot_nn(weight, values) * inv).astype(BF16)
            for h in range(3):
                s["mixed"][b, :, pl.ds(64 * (3 * g + h), 64)] = mixed[128 * h : 128 * h + 128]

    have_all("a2", a2)
    w_out = a2[...].reshape(DP_ROWS, D)
    s["mixed_spread"][...] = dot_nn(s["mixed"][...].reshape(256, D), s["spread"][...]).astype(BF16)
    middle = x_ref[...].reshape(256, D).astype(F32) + dot_nn(s["mixed_spread"][...], w_out)
    s["middle"][...] = middle
    inv2 = lax.rsqrt(jnp.sum(middle * middle, axis=1, keepdims=True) * (1.0 / D) + NORM_EPS)
    s["inv2"][...] = inv2
    s["n2"][0] = (middle * inv2 * s["gain2"][...]).astype(BF16)
    net.start(n2_slot, s["n2"].at[0], s["n2"].at[1], place.other_core())
    net.arrived(dy_slot, s["dy"].at[1], place.other_core())
    net.arrived(n2_slot, s["n2"].at[1], place.other_core())

    rs_slots = [[[net.new() for _ in range(3)] for _ in range(3)] for _ in range(3)]
    normed, upper = s["n2"][...].reshape(512, D), s["dy"][...].reshape(512, D)
    for p in range(3):
        ff_have(p)
        w_gate, w_up, w_down = (
            s["w"][p, :, :, pl.ds(16 * t, 16), :].reshape(256, D) for t in range(3)
        )
        gate = dot_nt(normed, w_gate)
        up = dot_nt(normed, w_up)
        d_act = dot_nt(upper, w_down)
        sigmoid = 1.0 / (1.0 + jnp.exp(-gate))
        silu = gate * sigmoid
        act = (silu * up).astype(BF16)
        d_gate = (d_act * up * sigmoid * (1.0 + gate * (1.0 - sigmoid))).astype(BF16)
        d_up = (d_act * silu).astype(BF16)
        back = dot_nn(d_gate, w_gate) + dot_nn(d_up, w_up)
        ahead = dot_nn(act, w_down)
        if p == 0:
            s["dn2"][...] = back
            s["ahead"][...] = ahead
        else:
            s["dn2"][...] += back
            s["ahead"][...] += ahead
        for t, (left, right) in enumerate(((d_gate, normed), (d_up, normed), (act, upper))):
            s["g"][p, :, :, pl.ds(16 * t, 16), :] = (
                dot_tn(left, right).astype(BF16).reshape(4, 4, 16, D)
            )
        three = ORDERS[p][2]
        last = place.coordinate(three)
        for d in (1, 2, 3):
            net.start(
                rs_slots[p][0][d - 1],
                s["g"].at[p, (last + d) % 4],
                s["ra"].at[p, d - 1],
                place.ring(three, d),
            )
    s["dn2_out"][...] = s["dn2"][pl.ds(256, 256)].astype(BF16)
    net.start(dn2_slot, s["dn2_out"], s["dn2_in"], place.other_core())
    s["ahead_out"][...] = s["ahead"][pl.ds(256, 256)].astype(BF16)
    net.start(out_slot, s["ahead_out"], s["ahead_in"], place.other_core())

    def rs_second():
        for p, (_, two, three) in enumerate(ORDERS):
            for d in (1, 2, 3):
                net.arrived(rs_slots[p][0][d - 1], s["ra"].at[p, d - 1], place.ring(three, -d))
            total = s["g"][p, place.coordinate(three)].astype(F32)
            for d in range(3):
                total += s["ra"][p, d].astype(F32)
            s["s2"][p] = total.astype(BF16)
            mine = place.coordinate(two)
            for d in (1, 2, 3):
                net.start(
                    rs_slots[p][1][d - 1],
                    s["s2"].at[p, (mine + d) % 4],
                    s["rb"].at[p, d - 1],
                    place.ring(two, d),
                )

    def rs_third():
        for p, (one, two, _) in enumerate(ORDERS):
            for d in (1, 2, 3):
                net.arrived(rs_slots[p][1][d - 1], s["rb"].at[p, d - 1], place.ring(two, -d))
            total = s["s2"][p, place.coordinate(two)].astype(F32)
            for d in range(3):
                total += s["rb"][p, d].astype(F32)
            s["u"][p] = dot_nn(unpack, total.astype(BF16)).astype(BF16).reshape(4, 16, D)
            mine = place.coordinate(one)
            for d in (1, 2, 3):
                net.start(
                    rs_slots[p][2][d - 1],
                    s["u"].at[p, (mine + d) % 4],
                    s["rc"].at[p, d - 1],
                    place.ring(one, d),
                )

    def rs_result():
        for p, (one, _, _) in enumerate(ORDERS):
            for d in (1, 2, 3):
                net.arrived(rs_slots[p][2][d - 1], s["rc"].at[p, d - 1], place.ring(one, -d))
            total = s["u"][p, place.coordinate(one)].astype(F32)
            for d in range(3):
                total += s["rc"][p, d].astype(F32)
            s["f"][pl.ds(16 * p, 16)] = total

    net.arrived(dn2_slot, s["dn2_in"], place.other_core())
    d_normed = s["dn2"][pl.ds(0, 256)] + s["dn2_in"][...].astype(F32)
    middle, inv2 = s["middle"][...], s["inv2"][...]
    unit2 = middle * inv2
    scaled = d_normed * s["gain2"][...]
    inner = jnp.sum(scaled * unit2, axis=1, keepdims=True) * (1.0 / D)
    d_middle = s["dy"][0].astype(F32) + inv2 * (scaled - unit2 * inner)
    s["d_middle"][...] = d_middle
    g_gain2 = jnp.sum(d_normed * unit2, axis=0, keepdims=True)
    d_branch = d_middle.astype(BF16)
    w_out = a2[...].reshape(DP_ROWS, D)
    d_mixed = dot_nt(d_branch, w_out).astype(BF16)
    s["d_mixed"][...] = dot_nt(d_mixed, s["spread"][...]).astype(BF16).reshape(2, 128, D)
    out_sum = Summed(net, place, s["sum_out"])
    grad = dot_tn(s["mixed_spread"][...], d_branch).astype(BF16).reshape(8, 2, PAD, D)
    for c in range(2):
        s["sum_out"][0][c] = grad[:, c]
    out_sum.begin()

    dkv_slots = [[net.new() for _ in range(7)] for _ in range(2)]
    dkv_copies = []
    for b in range(2):
        for g in range(3):
            inv = s["inv_sum"][b, g]
            keys = s["kv"][:, b, :, pl.ds(64 * g, 64)].reshape(1024, 64)
            values = s["kv"][:, b, :, pl.ds(192 + 64 * g, 64)].reshape(1024, 64)
            query = heads(s["q"][b], g)
            d_out = (heads(s["d_mixed"][b], g).astype(F32) * inv).astype(BF16)
            inner = jnp.sum(
                d_out.astype(F32) * heads(s["mixed"][b], g).astype(F32), axis=1, keepdims=True
            )
            weight = s["attn"][b, g]
            d_score = (weight.astype(F32) * (dot_nt(d_out, values) - inner)).astype(BF16)
            d_query = dot_nn(d_score, keys) * HEAD_WIDTH**-0.5
            for h in range(3):
                s["dq"][b, :, pl.ds(64 * (3 * g + h), 64)] = d_query[128 * h : 128 * h + 128]
            d_keys = jnp.transpose(dot_tn(query, d_score)).astype(BF16)
            d_values = jnp.transpose(dot_tn(d_out, weight)).astype(BF16)
            s["dkv"][:, b, :, pl.ds(64 * g, 64)] = d_keys.reshape(8, 128, 64)
            s["dkv"][:, b, :, pl.ds(192 + 64 * g, 64)] = d_values.reshape(8, 128, 64)
        for k in range(1, 8):
            copy = net.copy(
                dkv_slots[b][k - 1], s["dkv"].at[k, b], s["dkv_in"].at[k, b], place.rank(-k)
            )
            dkv_copies.append((k, copy))
            pl.when(k <= rank)(copy.start)
        if b == 0:
            out_sum.over_group()
            rs_second()
    net.arrived(out_slot, s["ahead_in"], place.other_core())
    out = s["middle"][...] + s["ahead"][pl.ds(0, 256)] + s["ahead_in"][...].astype(F32)
    out_ref[...] = out.astype(BF16).reshape(2, 128, D)

    cos, sin = s["cos"][...], s["sin"][...]
    lane = iota((256, 128), 1)
    for t in range(5):
        if t < 4:
            tile = s["dq"][:, :, pl.ds(128 * t, 128)].reshape(256, 128)
        else:
            tile = s["dq"][:, :, pl.ds(512, 64)].reshape(256, 64)
            tile = jnp.concatenate([tile, jnp.zeros((256, 64), F32)], axis=1)
        tile = tile * cos - swap_halves(tile) * sin
        s["dqkv"][:, pl.ds(384 + 128 * t, 128)] = tile.astype(BF16)
    n1 = s["n1"][...]
    q_sum = Summed(net, place, s["sum_q"])
    grad = dot_tn(n1, s["dqkv"][:, pl.ds(384, 512)]).astype(BF16).reshape(8, 2, PAD, 512)
    for c in range(2):
        s["sum_q"][0][c] = grad[:, c]
    q_sum.begin()
    out_sum.over_ranks()
    rs_third()
    q_sum.over_group()

    for b in range(2):
        s["dkv_sum"][b] = s["dkv"][0, b].astype(F32)
    for k in range(1, 8):

        @pl.when(rank + k <= 7)
        def _(k=k):
            for b in range(2):
                net.arrived(dkv_slots[b][k - 1], s["dkv_in"].at[k, b], place.rank(k))
            s["dkv_sum"][...] += s["dkv_in"][k].astype(F32)

    for t in range(3):
        tile = s["dkv_sum"][:, :, pl.ds(128 * t, 128)].reshape(256, 128)
        if t < 2:
            turned = tile * cos - swap_halves(tile) * sin
            tile = jnp.where(lane < 64, turned, tile) if t == 1 else turned
        s["dqkv"][:, pl.ds(128 * t, 128)] = tile.astype(BF16)
    d_pre = s["dqkv"][...]
    d_normed = dot_nt(d_pre, a1[...].reshape(DP_ROWS, 1024))
    unit1 = s["unit1"][...]
    g_gain1 = jnp.sum(d_normed * unit1, axis=0, keepdims=True)
    spread = s["spread"][...]
    g_gain2 = dot_nn(jnp.broadcast_to(g_gain2, (16, D)).astype(BF16), spread)[0:1]
    row = iota((128, DP_ROWS), 0)
    g_gains = jnp.transpose(jnp.where(row == 64, g_gain1, jnp.where(row == 65, g_gain2, 0.0)))
    t_sum = Summed(net, place, s["sum_t"])
    grad = dot_tn(n1, d_pre[:, 0:384]).astype(BF16).reshape(8, 2, PAD, 384)
    rest = dot_tn(n1, d_pre[:, 896:1024]) + g_gains
    rest = rest.astype(BF16).reshape(8, 2, PAD, 128)
    for c in range(2):
        s["sum_t"][0][c, :, :, pl.ds(0, 384)] = grad[:, c]
        s["sum_t"][0][c, :, :, pl.ds(384, 128)] = rest[:, c]
    t_sum.begin()

    scaled = d_normed * s["gain1"][...]
    inner = jnp.sum(scaled * unit1, axis=1, keepdims=True) * (1.0 / D)
    d_in = s["inv1"][...] * (scaled - unit1 * inner)
    high = d_in.astype(BF16)
    low = (d_in - high.astype(F32)).astype(BF16)
    d_in = s["d_middle"][...] + dot_nt(high, spread) + dot_nt(low, spread)
    gx_ref[...] = d_in.astype(BF16).reshape(2, 128, D)

    t_sum.over_group()
    q_sum.over_ranks()
    rs_result()
    sums = s["f"][...]
    high = sums.astype(BF16)
    low = (sums - high.astype(F32)).astype(BF16)
    row, col = iota((PAD, 12), 0), iota((PAD, 12), 1)
    for t, ref in enumerate((gg_ref, gu_ref)):
        pick = one_hot(row == ((col >> 2) << 4) + 4 * t + (col & 3))
        ref[...] = dot_tn(high, pick) + dot_tn(low, pick)
    row, col = iota((12, PAD), 0), iota((12, PAD), 1)
    pick = one_hot(col == ((row >> 2) << 4) + 8 + (row & 3))
    gd_ref[...] = dot_nn(pick, high) + dot_nn(pick, low)
    go_ref[...] = out_sum.result()[0:ROWS]
    t_sum.over_ranks()
    total = q_sum.result()
    gq_ref[:, pl.ds(0, 512)] = total[0:ROWS]
    total = t_sum.result()
    gk_ref[...] = total[0:ROWS, 0:192]
    gv_ref[...] = total[0:ROWS, 192:384]
    gq_ref[:, pl.ds(512, 64)] = total[0:ROWS, 384:448]
    across = jnp.transpose(total[:, 384:512])
    gna_ref[...] = across[64:65, 0:ROWS]
    gnm_ref[...] = across[65:66, 0:ROWS]

    net.finish()
    for k, copy in enumerate(kv_copies, 1):
        pl.when(rank + k <= 7)(copy.wait_send)
    for k, copy in dkv_copies:
        pl.when(k <= rank)(copy.wait_send)


def sum_buffers(width):
    return [
        pltpu.VMEM((2, 8, PAD, width), BF16),
        pltpu.VMEM((8, PAD, width), BF16),
        pltpu.VMEM((8, PAD, width), BF16),
        pltpu.VMEM((7, PAD, width), BF16),
        pltpu.VMEM((PAD, width), BF16),
        pltpu.VMEM((7, PAD, width), BF16),
    ]


COPIES = 160

SCRATCH = {
    "send": pltpu.SemaphoreType.DMA((COPIES,)),
    "recv": pltpu.SemaphoreType.DMA((COPIES,)),
    "tile": pltpu.VMEM((3, 16, D), BF16),
    "first": pltpu.VMEM((3, 4, 16, D), BF16),
    "w": pltpu.VMEM((3, 4, 4, PAD, D), BF16),
    "a1": pltpu.VMEM((BLOCKS, PAD, 1024), BF16),
    "a2": pltpu.VMEM((BLOCKS, PAD, D), BF16),
    "spread": pltpu.VMEM((D, DP_ROWS), BF16),
    "cos": pltpu.VMEM((256, 128), F32),
    "sin": pltpu.VMEM((256, 128), F32),
    "bias": pltpu.VMEM((2, 128, 1024), F32),
    "inv1": pltpu.VMEM((256, 1), F32),
    "unit1": pltpu.VMEM((256, DP_ROWS), F32),
    "gain1": pltpu.VMEM((1, DP_ROWS), F32),
    "gain2": pltpu.VMEM((1, D), F32),
    "n1": pltpu.VMEM((256, DP_ROWS), BF16),
    "q": pltpu.VMEM((2, 128, 640), BF16),
    "kv": pltpu.VMEM((8, 2, 128, 384), BF16),
    "attn": pltpu.VMEM((2, 3, 384, 1024), BF16),
    "inv_sum": pltpu.VMEM((2, 3, 384, 1), F32),
    "mixed": pltpu.VMEM((2, 128, D), BF16),
    "mixed_spread": pltpu.VMEM((256, DP_ROWS), BF16),
    "middle": pltpu.VMEM((256, D), F32),
    "inv2": pltpu.VMEM((256, 1), F32),
    "n2": pltpu.VMEM((2, 256, D), BF16),
    "dy": pltpu.VMEM((2, 256, D), BF16),
    "dn2": pltpu.VMEM((512, D), F32),
    "ahead": pltpu.VMEM((512, D), F32),
    "dn2_out": pltpu.VMEM((256, D), BF16),
    "dn2_in": pltpu.VMEM((256, D), BF16),
    "ahead_out": pltpu.VMEM((256, D), BF16),
    "ahead_in": pltpu.VMEM((256, D), BF16),
    "d_middle": pltpu.VMEM((256, D), F32),
    "d_mixed": pltpu.VMEM((2, 128, D), BF16),
    "dq": pltpu.VMEM((2, 128, D), F32),
    "dkv": pltpu.VMEM((8, 2, 128, 384), BF16),
    "dkv_in": pltpu.VMEM((8, 2, 128, 384), BF16),
    "dkv_sum": pltpu.VMEM((2, 128, 384), F32),
    "dqkv": pltpu.VMEM((256, 1024), BF16),
    "g": pltpu.VMEM((3, 4, 4, PAD, D), BF16),
    "ra": pltpu.VMEM((3, 3, 4, PAD, D), BF16),
    "s2": pltpu.VMEM((3, 4, PAD, D), BF16),
    "rb": pltpu.VMEM((3, 3, PAD, D), BF16),
    "u": pltpu.VMEM((3, 4, 16, D), BF16),
    "rc": pltpu.VMEM((3, 3, 16, D), BF16),
    "f": pltpu.VMEM((PAD, D), F32),
    "sum_out": sum_buffers(D),
    "sum_q": sum_buffers(512),
    "sum_t": sum_buffers(512),
}


def local(
    inputs, segment_ids, norm_attn, w_query, w_key, w_value, w_out, norm_mlp, w_gate, w_up, w_down, cotangent,
):
    columns = [w_key, w_value, w_query, norm_attn[:, None], norm_mlp[:, None]]
    a1 = jnp.pad(jnp.concatenate(columns, axis=1), ((0, PAD - ROWS), (0, 62)))
    a2 = jnp.pad(w_out, ((0, PAD - ROWS), (0, 0)))
    half = HEAD_WIDTH // 2
    freq = ROPE_BASE ** (-(2.0 * jnp.arange(half, dtype=F32)) / HEAD_WIDTH)
    freq = jnp.tile(freq, 4)[None, :]
    shapes = [
        ((2, 128, D), BF16),
        ((2, 128, D), BF16),
        ((1, ROWS), F32),
        ((ROWS, 576), F32),
        ((ROWS, 192), F32),
        ((ROWS, 192), F32),
        ((ROWS, D), F32),
        ((1, ROWS), F32),
        ((D, 12), F32),
        ((D, 12), F32),
        ((12, D), F32),
    ]
    outs = pl.pallas_call(
        kernel,
        out_shape=[jax.ShapeDtypeStruct(shape, dtype) for shape, dtype in shapes],
        in_specs=[pl.BlockSpec(memory_space=pltpu.VMEM)] * 9,
        out_specs=[pl.BlockSpec(memory_space=pltpu.VMEM)] * len(shapes),
        scratch_shapes=[SCRATCH],
        compiler_params=pltpu.CompilerParams(
            collective_id=0, has_side_effects=True, vmem_limit_bytes=60 * 2**20
        ),
        name="layer",
    )(inputs, segment_ids, a1, a2, w_gate, w_up, w_down, cotangent, freq)
    outs = list(outs)
    outs[2], outs[7] = outs[2].reshape(ROWS), outs[7].reshape(ROWS)
    return tuple(outs)


def solution(mesh):
    rows, both = P("dp", None), ("dp", "seq")
    tokens = P("dp", "seq", None)
    weights = (P("dp"), rows, rows, rows, rows, P("dp"), P(None, both), P(None, both), P(both, None))
    return jax.shard_map(
        local,
        mesh=mesh,
        in_specs=(tokens, P("dp", None), *weights, tokens),
        out_specs=(tokens, tokens, *weights),
        check_vma=False,
    )
```

```python
import functools

import jax
import jax.numpy as jnp
import numpy as np
from jax import lax
from jax.experimental import pallas as pl
from jax.experimental.pallas import tpu as pltpu
from jax.sharding import PartitionSpec as P

MESH = pl.DeviceIdType.MESH
F32 = jnp.float32
BF16 = jnp.bfloat16

D = 576
FF = 1536
QUERY_HEADS = 9
KV_HEADS = 3
HEAD_WIDTH = 64
ROPE_BASE = 100000.0
NORM_EPS = 1e-05
MASKED = -1e30

ROWS = 36
PAD = 48
BLOCKS = 16
DP_ROWS = BLOCKS * PAD
ORDERS = (("x", "y", "z"), ("y", "z", "x"), ("z", "x", "y"))
BACK = (("z", "y"), ("z", "x"), ("x", "y"))


def dot_nn(a, b):
    return lax.dot_general(a, b, (((1,), (0,)), ((), ())), preferred_element_type=F32)


def dot_nt(a, b):
    return lax.dot_general(a, b, (((1,), (1,)), ((), ())), preferred_element_type=F32)


def dot_tn(a, b):
    return lax.dot_general(a, b, (((0,), (0,)), ((), ())), preferred_element_type=F32)


def iota(shape, dim):
    return lax.broadcasted_iota(jnp.int32, shape, dim)


def one_hot(cond):
    return jnp.where(cond, 1.0, 0.0).astype(BF16)


class Place:
    def __init__(self):
        self.dp = lax.axis_index("dp")
        self.seq = lax.axis_index("seq")
        self.z = self.dp // 4
        self.x_hi = (self.dp // 2) % 2
        self.core = self.dp % 2
        self.y = self.seq // 2
        self.x_lo = self.seq % 2
        self.x = 2 * self.x_hi + self.x_lo

    def at(self, x, y, z, core):
        return (z * 4 + (x // 2) * 2 + core, y * 2 + x % 2)

    def coordinate(self, axis):
        return {"x": self.x, "y": self.y, "z": self.z}[axis]

    def ring(self, axis, step):
        here = {"x": self.x, "y": self.y, "z": self.z}
        here[axis] = (here[axis] + step + 4) % 4
        return self.at(here["x"], here["y"], here["z"], self.core)

    def other_core(self):
        return (self.dp + 1 - 2 * self.core, self.seq)

    def group(self, dz, dx):
        z = (self.z + dz + 4) % 4
        x = 3 - self.x if dx else self.x
        return self.at(x, self.y, z, self.core), z * 2 + x // 2

    def pair(self):
        return self.at(self.x + 1 - 2 * self.x_lo, self.y, self.z, self.core)

    def rank(self, step):
        return (self.dp, (self.seq + step + 8) % 8)


class Net:
    def __init__(self, send, recv):
        self.send, self.recv, self.used = send, recv, 0
        self.unsent, self.maybe_unsent = [], []

    def new(self):
        self.used += 1
        return self.used - 1

    def copy(self, slot, src, dst, device):
        return pltpu.make_async_remote_copy(
            src_ref=src,
            dst_ref=dst,
            send_sem=self.send.at[slot],
            recv_sem=self.recv.at[slot],
            device_id=device,
            device_id_type=MESH,
        )

    def start(self, slot, src, dst, device):
        copy = self.copy(slot, src, dst, device)
        copy.start()
        self.unsent.append(copy)

    def arrived(self, slot, dst, device):
        self.copy(slot, dst, dst, device).wait_recv()

    def start_if(self, wanted, slot, src, dst, device):
        copy = self.copy(slot, src, dst, device)
        pl.when(wanted)(copy.start)
        self.maybe_unsent.append((wanted, copy))

    def arrived_if(self, wanted, slot, dst, device):
        pl.when(wanted)(functools.partial(self.arrived, slot, dst, device))

    def finish(self):
        for copy in self.unsent:
            copy.wait_send()
        for wanted, copy in self.maybe_unsent:
            pl.when(wanted)(copy.wait_send)


GROUP_STEPS = [(dz, dx) for dz in range(4) for dx in range(2) if (dz, dx) != (0, 0)]


class Summed:
    def __init__(self, net, place, refs):
        self.net, self.place = net, place
        self.mine, self.from_core, self.chip, self.from_group, self.one, self.from_rank = refs
        self.core_slot = net.new()
        self.group_slots = [net.new() for _ in GROUP_STEPS]
        self.rank_slots = [net.new() for _ in range(7)]

    def fill(self, first, value):
        width = value.shape[1]
        value = value.astype(BF16).reshape(8, 2, PAD, width)
        for c in range(2):
            self.mine[c, :, :, pl.ds(first, width)] = value[:, c]

    def begin(self):
        place = self.place
        self.net.start(
            self.core_slot, self.mine.at[1 - place.core], self.from_core, place.other_core()
        )

    def over_group(self):
        place, net = self.place, self.net
        net.arrived(self.core_slot, self.from_core, place.other_core())
        self.chip[...] = (
            self.mine[place.core].astype(F32) + self.from_core[...].astype(F32)
        ).astype(BF16)
        for k, (dz, dx) in enumerate(GROUP_STEPS):
            device, index = place.group(dz, dx)
            net.start(self.group_slots[k], self.chip.at[index], self.from_group.at[k], device)

    def over_ranks(self):
        place, net = self.place, self.net
        for k, (dz, dx) in enumerate(GROUP_STEPS):
            device, _ = place.group(-dz, dx)
            net.arrived(self.group_slots[k], self.from_group.at[k], device)
        total = self.chip[place.z * 2 + place.x_hi].astype(F32)
        for k in range(7):
            total += self.from_group[k].astype(F32)
        self.one[...] = total.astype(BF16)
        for k in range(7):
            net.start(self.rank_slots[k], self.one, self.from_rank.at[k], place.rank(k + 1))

    def result(self):
        place, net = self.place, self.net
        for k in range(7):
            net.arrived(self.rank_slots[k], self.from_rank.at[k], place.rank(-k - 1))
        total = self.one[...].astype(F32)
        for k in range(7):
            total += self.from_rank[k].astype(F32)
        return total


class SplitSummed:
    def __init__(self, net, place, refs):
        self.net, self.place = net, place
        (
            self.mine, self.from_core, self.chip, self.from_y, self.part, self.from_group, self.one, self.from_pair,
            self.whole,
        ) = refs
        self.core_slot, self.pair_slot = net.new(), net.new()
        self.y_slots = [net.new() for _ in range(3)]
        self.group_slots = [net.new() for _ in GROUP_STEPS]
        self.back_slots = [net.new() for _ in range(3)]

    def fill(self, value):
        value = value.astype(BF16)
        for t in range(4):
            tile = value[:, 128 * t : 128 * t + 128].reshape(8, 2, PAD, 128)
            for c in range(2):
                self.mine[c, t] = tile[:, c]

    def begin(self):
        place = self.place
        self.net.start(
            self.core_slot, self.mine.at[1 - place.core], self.from_core, place.other_core()
        )

    def over_y(self):
        place, net = self.place, self.net
        net.arrived(self.core_slot, self.from_core, place.other_core())
        self.chip[...] = (
            self.mine[place.core].astype(F32) + self.from_core[...].astype(F32)
        ).astype(BF16)
        for d in (1, 2, 3):
            net.start(
                self.y_slots[d - 1],
                self.chip.at[(place.y + d) % 4],
                self.from_y.at[d - 1],
                place.ring("y", d),
            )

    def over_group(self):
        place, net = self.place, self.net
        for d in (1, 2, 3):
            net.arrived(self.y_slots[d - 1], self.from_y.at[d - 1], place.ring("y", -d))
        total = self.chip[place.y].astype(F32)
        for d in range(3):
            total += self.from_y[d].astype(F32)
        self.part[...] = total.astype(BF16)
        for k, (dz, dx) in enumerate(GROUP_STEPS):
            device, index = place.group(dz, dx)
            net.start(self.group_slots[k], self.part.at[index], self.from_group.at[k], device)

    def over_pair(self):
        place, net = self.place, self.net
        for k, (dz, dx) in enumerate(GROUP_STEPS):
            device, _ = place.group(-dz, dx)
            net.arrived(self.group_slots[k], self.from_group.at[k], device)
        total = self.part[place.z * 2 + place.x_hi].astype(F32)
        for k in range(7):
            total += self.from_group[k].astype(F32)
        self.one[...] = total.astype(BF16)
        net.start(self.pair_slot, self.one, self.from_pair, place.pair())

    def back(self):
        place, net = self.place, self.net
        net.arrived(self.pair_slot, self.from_pair, place.pair())
        total = self.one[...].astype(F32) + self.from_pair[...].astype(F32)
        self.whole[place.y] = total.astype(BF16)
        for d in (1, 2, 3):
            tile = self.whole.at[place.y]
            net.start(self.back_slots[d - 1], tile, tile, place.ring("y", d))

    def result(self, ref):
        place, net = self.place, self.net
        for d in (1, 2, 3):
            net.arrived(
                self.back_slots[d - 1], self.whole.at[(place.y + 4 - d) % 4], place.ring("y", -d)
            )
        for t in range(4):
            ref[:, pl.ds(128 * t, 128)] = self.whole[t, pl.ds(0, ROWS)].astype(F32)


class Gathered:
    def __init__(self, net, place, whole):
        self.net, self.place, self.whole = net, place, whole
        self.group_slots = [net.new() for _ in GROUP_STEPS]
        self.core_slots = [net.new() for _ in range(8)]

    def begin(self):
        place, net = self.place, self.net
        block = self.whole.at[place.dp]
        for k, (dz, dx) in enumerate(GROUP_STEPS):
            net.start(self.group_slots[k], block, block, place.group(dz, dx)[0])
        net.start(self.core_slots[7], block, block, place.other_core())

    def pass_on(self):
        place, net = self.place, self.net
        for k, (dz, dx) in enumerate(GROUP_STEPS):
            device, index = place.group(-dz, dx)
            block = self.whole.at[index * 2 + place.core]
            net.arrived(self.group_slots[k], block, device)
            net.start(self.core_slots[k], block, block, place.other_core())

    def finish(self):
        place, net = self.place, self.net
        for k, (dz, dx) in enumerate(GROUP_STEPS):
            _, index = place.group(-dz, dx)
            block = self.whole.at[index * 2 + 1 - place.core]
            net.arrived(self.core_slots[k], block, place.other_core())
        net.arrived(self.core_slots[7], self.whole.at[place.other_core()[0]], place.other_core())


def swap_halves(tile):
    first = (iota(tile.shape, 1) & 32) == 0
    return jnp.where(first, pltpu.roll(tile, 96, 1), pltpu.roll(tile, 32, 1))


def kernel(
    x_ref, seg_ref, na_ref, wq_ref, wk_ref, wv_ref, wo_ref, nm_ref, wg_ref, wu_ref, wd_ref, dy_ref, freq_ref,
    out_ref, gx_ref, gna_ref, gq_ref, gk_ref, gv_ref, go_ref, gnm_ref, gg_ref, gu_ref, gd_ref,
    s,
):
    place = Place()
    net = Net(s["send"], s["recv"])
    rank = place.seq

    barrier = pltpu.get_barrier_semaphore()
    peers = [place.ring(axis, step) for axis in "xyz" for step in (1, 2, 3)]
    peers += [place.other_core()]
    peers += [place.group(dz, 1)[0] for dz in (1, 2, 3)]
    flipped = place.x + 1 - 2 * place.x_lo
    peers += [place.at(flipped, (place.y + dy) % 4, place.z, place.core) for dy in (1, 2, 3)]
    for peer in peers:
        pl.semaphore_signal(barrier, inc=1, device_id=peer, device_id_type=MESH)

    a1, a2 = s["a1"], s["a2"]
    down = one_hot(iota((PAD, ROWS), 0) == iota((PAD, ROWS), 1))
    keys, values = dot_nn(down, wk_ref[...]), dot_nn(down, wv_ref[...])
    a1[place.dp, :, pl.ds(0, 384)] = jnp.concatenate([keys, values], axis=1).astype(BF16)
    query = dot_nn(down, wq_ref[...])
    a1[place.dp, :, pl.ds(384, 512)] = query[:, 0:512].astype(BF16)
    row = iota((128, ROWS), 0)
    gains = jnp.where(row == 64, na_ref[...], jnp.where(row == 65, nm_ref[...], 0.0)).astype(BF16)
    tail = jnp.concatenate([query[:, 512:576], jnp.zeros((PAD, 64), F32)], axis=1)
    a1[place.dp, :, pl.ds(896, 128)] = (tail + dot_nt(down, gains)).astype(BF16)
    a2[place.dp] = dot_nn(down, wo_ref[...]).astype(BF16)

    row, col = iota((16, 12), 0), iota((16, 12), 1)
    for p in range(3):
        tile = jnp.zeros((16, D), F32)
        for t, ref in enumerate((wg_ref, wu_ref, wd_ref)):
            pick = one_hot(((row >> 2) == t) & (col == 4 * p + (row & 3)))
            tile += dot_nn(pick, ref[...])
        s["tile"][p] = tile.astype(BF16)

    pl.semaphore_wait(barrier, len(peers))

    first_weights, out_weights = Gathered(net, place, a1), Gathered(net, place, a2)
    ff_slots = [[[net.new() for _ in range(3)] for _ in range(3)] for _ in range(3)]
    dy_slot, n2_slot, out_slot, dn2_slot = (net.new() for _ in range(4))
    first_weights.begin()
    for p, (one, _, _) in enumerate(ORDERS):
        mine = place.coordinate(one)
        s["first"][p, mine] = s["tile"][p]
        for d in (1, 2, 3):
            net.start(
                ff_slots[p][0][d - 1], s["tile"].at[p], s["first"].at[p, mine], place.ring(one, d)
            )
    for b in range(2):
        s["x"][pl.ds(128 * b, 128)] = jnp.transpose(x_ref[b].astype(F32)).astype(BF16)
        s["dy"][0, pl.ds(128 * b, 128)] = jnp.transpose(dy_ref[b].astype(F32)).astype(BF16)
    net.start(dy_slot, s["dy"].at[0], s["dy"].at[1], place.other_core())

    row = iota((D, DP_ROWS), 0).astype(F32)
    col = iota((D, DP_ROWS), 1).astype(F32)
    s["spread"][...] = one_hot(col - row == 12.0 * jnp.floor((row + 0.5) * (1.0 / ROWS)))
    lane = iota((128, 128), 1)
    for b in range(2):
        own = seg_ref[pl.ds(b, 1), pl.ds(pl.multiple_of(rank * 128, 128), 128)].astype(F32)
        own = jnp.transpose(jnp.broadcast_to(own, (128, 128)))
        earlier = jnp.zeros((128, 128), F32)
        for c in range(8):
            part = seg_ref[pl.ds(b, 1), pl.ds(128 * c, 128)].astype(F32)
            earlier += jnp.where(part < own, 1.0, 0.0)
        begin = jnp.sum(earlier, axis=1, keepdims=True)
        here = (iota((128, 1), 0) + rank * 128).astype(F32)
        angle = (here - begin) * freq_ref[...]
        s["cos"][pl.ds(128 * b, 128)] = jnp.cos(angle)
        sine = jnp.sin(angle)
        s["sin"][pl.ds(128 * b, 128)] = jnp.where((lane & 32) == 0, -sine, sine)
        for k in range(8):
            key = (lane + 128 * (rank - k)).astype(F32)
            s["bias"][b, :, pl.ds(128 * k, 128)] = jnp.where(
                (key >= begin) & (key <= here), 0.0, MASKED
            )
    x = s["x"][...]
    x32 = x.astype(F32)
    inv1 = lax.rsqrt(jnp.sum(x32 * x32, axis=1, keepdims=True) * (1.0 / D) + NORM_EPS)
    s["inv1"][...] = inv1
    s["unit1"][...] = dot_nn(x, s["spread"][...]) * inv1
    for k in range(1, 8):

        @pl.when(k > rank)
        def _(k=k):
            s["kv"][k] = jnp.zeros((2, 128, 384), BF16)

    row, col = iota((PAD, 64), 0), iota((PAD, 64), 1)
    pack = one_hot(col == (((row >> 2) & 3) << 4) + ((row >> 4) << 2) + (row & 3))
    row, col = iota((64, PAD), 0), iota((64, PAD), 1)
    unpack = one_hot(row == (((col >> 2) & 3) << 4) + ((col >> 4) << 2) + (col & 3))

    def ff_second():
        for p, (one, two, three) in enumerate(ORDERS):
            mine = place.coordinate(one)
            for d in (1, 2, 3):
                net.arrived(
                    ff_slots[p][0][d - 1], s["first"].at[p, (mine + 4 - d) % 4], place.ring(one, -d)
                )
            block = s["w"].at[p, place.coordinate(three), place.coordinate(two)]
            block[...] = dot_nn(pack, s["first"][p].reshape(64, D)).astype(BF16)
            for d in (1, 2, 3):
                net.start(ff_slots[p][1][d - 1], block, block, place.ring(two, d))

    def ff_third(p):
        _, two, three = ORDERS[p]
        mine, last = place.coordinate(two), place.coordinate(three)
        for d in (1, 2, 3):
            net.arrived(
                ff_slots[p][1][d - 1], s["w"].at[p, last, (mine + 4 - d) % 4], place.ring(two, -d)
            )
        block = s["w"].at[p, last]
        for d in (1, 2, 3):
            net.start(ff_slots[p][2][d - 1], block, block, place.ring(three, d))

    def ff_have(p):
        three = ORDERS[p][2]
        last = place.coordinate(three)
        for d in (1, 2, 3):
            net.arrived(
                ff_slots[p][2][d - 1], s["w"].at[p, (last + 4 - d) % 4], place.ring(three, -d)
            )

    ff_second()
    first_weights.pass_on()
    first_weights.finish()

    gains = jnp.transpose(a1[:, :, pl.ds(896, 128)].reshape(DP_ROWS, 128).astype(F32))
    gain1 = gains[64:65]
    s["gain1"][...] = gain1
    gain2 = dot_nt(gains[64:80].astype(BF16), s["spread"][...])[1:2]
    s["gain2"][...] = gain2
    s["n1"][...] = (s["unit1"][...] * gain1).astype(BF16)
    pre = dot_nn(s["n1"][...], a1[...].reshape(DP_ROWS, 1024))
    cos, sin = s["cos"][...], s["sin"][...]
    lane = iota((256, 128), 1)
    for t in range(8):
        tile = pre[:, 128 * t : 128 * t + 128]
        if t != 2:
            turned = tile * cos + swap_halves(tile) * sin
            tile = jnp.where(lane < 64, turned, tile) if t == 1 else turned
        if t < 3:
            s["kv"][0, :, :, pl.ds(128 * t, 128)] = tile.astype(BF16).reshape(2, 128, 128)
        else:
            tile = (tile * HEAD_WIDTH**-0.5).astype(BF16).reshape(2, 128, 128)
            s["q"][:, :, pl.ds(128 * t - 384, 128)] = tile

    kv, apart = s["kv"], place.x_lo == 0
    kv_slots = [net.new() for _ in range(8)]
    column_slots = [net.new() for _ in range(8)]
    across_slots = [net.new() for _ in range(8)]
    for k in (2, 4, 6):
        net.start_if(rank + k <= 7, column_slots[k], kv.at[0, 1], kv.at[k, 1], place.rank(k))
    net.start_if(apart, across_slots[1], kv.at[0, 1], kv.at[1, 1], place.pair())
    for k in range(1, 8):
        net.start_if(rank + k <= 7, kv_slots[k], kv.at[0, 0], kv.at[k, 0], place.rank(k))
    out_weights.begin()
    for k in (2, 6, 4):
        net.arrived_if(k <= rank, column_slots[k], kv.at[k, 1], place.rank(-k))
        here = k <= rank
        net.start_if(here & apart, across_slots[k + 1], kv.at[k, 1], kv.at[k + 1, 1], place.pair())
        net.start_if(
            here & jnp.logical_not(apart), across_slots[k - 1], kv.at[k, 1], kv.at[k - 1, 1], place.pair()
        )
    ff_third(0)
    out_weights.pass_on()
    for k in range(1, 8):
        net.arrived_if(k <= rank, kv_slots[k], kv.at[k, 0], place.rank(-k))
    for k in (1, 3, 5, 7):
        net.arrived_if(k <= rank, across_slots[k], kv.at[k, 1], place.pair())
    ff_third(1)
    ff_third(2)

    def heads(value, group):
        return jnp.concatenate(
            [value[:, 64 * h : 64 * h + 64] for h in range(3 * group, 3 * group + 3)], axis=0
        )

    @pl.loop(0, 2)
    def _(b):
        bias = s["bias"][b]
        for g in range(3):
            query = heads(s["q"][b], g)
            keys = s["kv"][:, b, :, pl.ds(64 * g, 64)].reshape(1024, 64)
            values = s["kv"][:, b, :, pl.ds(192 + 64 * g, 64)].reshape(1024, 64)
            score = (dot_nt(query, keys).reshape(3, 128, 1024) + bias[None]).reshape(384, 1024)
            top = jnp.max(score, axis=1, keepdims=True)
            score = jnp.exp(score - top)
            inv = 1.0 / jnp.sum(score, axis=1, keepdims=True)
            weight = score.astype(BF16)
            s["attn"][b, g] = weight
            s["inv_sum"][b, g] = inv
            mixed = (dot_nn(weight, values) * inv).astype(BF16)
            for h in range(3):
                s["mixed"][b, :, pl.ds(64 * (3 * g + h), 64)] = mixed[128 * h : 128 * h + 128]

    out_weights.finish()
    w_out = a2[...].reshape(DP_ROWS, D)
    s["mixed_spread"][...] = dot_nn(s["mixed"][...].reshape(256, D), s["spread"][...]).astype(BF16)
    middle = s["x"][...].astype(F32) + dot_nn(s["mixed_spread"][...], w_out)
    s["middle"][...] = middle
    inv2 = lax.rsqrt(jnp.sum(middle * middle, axis=1, keepdims=True) * (1.0 / D) + NORM_EPS)
    s["inv2"][...] = inv2
    s["n2"][0] = (middle * inv2 * s["gain2"][...]).astype(BF16)
    net.start(n2_slot, s["n2"].at[0], s["n2"].at[1], place.other_core())
    net.arrived(dy_slot, s["dy"].at[1], place.other_core())
    net.arrived(n2_slot, s["n2"].at[1], place.other_core())

    rs_slots = [[[net.new() for _ in range(3)] for _ in range(3)] for _ in range(3)]
    normed, upper = s["n2"][...].reshape(512, D), s["dy"][...].reshape(512, D)
    for p in (0, 2, 1):
        ff_have(p)
        w_gate, w_up, w_down = (
            s["w"][p, :, :, pl.ds(16 * t, 16), :].reshape(256, D) for t in range(3)
        )
        gate = dot_nt(normed, w_gate)
        up = dot_nt(normed, w_up)
        d_act = dot_nt(upper, w_down)
        sigmoid = 1.0 / (1.0 + jnp.exp(-gate))
        silu = gate * sigmoid
        act = (silu * up).astype(BF16)
        d_gate = (d_act * up * sigmoid * (1.0 + gate * (1.0 - sigmoid))).astype(BF16)
        d_up = (d_act * silu).astype(BF16)
        back = dot_nn(d_gate, w_gate) + dot_nn(d_up, w_up)
        ahead = dot_nn(act, w_down)
        if p == 0:
            s["dn2"][...] = back
            s["ahead"][...] = ahead
        else:
            s["dn2"][...] += back
            s["ahead"][...] += ahead
        for t, (left, right) in enumerate(((d_gate, normed), (d_up, normed), (act, upper))):
            s["g"][p, :, :, pl.ds(16 * t, 16), :] = (
                dot_tn(left, right).astype(BF16).reshape(4, 4, 16, D)
            )
        first = BACK[p][0]
        mine = place.coordinate(first)
        for d in (1, 2, 3):
            there = (mine + d) % 4
            net.start(
                rs_slots[p][0][d - 1],
                s["g"].at[p, there] if first == ORDERS[p][2] else s["g"].at[p, :, there],
                s["ra"].at[p, d - 1],
                place.ring(first, d),
            )
    s["dn2_out"][...] = s["dn2"][pl.ds(256, 256)].astype(BF16)
    net.start(dn2_slot, s["dn2_out"], s["dn2_in"], place.other_core())
    s["ahead_out"][...] = s["ahead"][pl.ds(256, 256)].astype(BF16)
    net.start(out_slot, s["ahead_out"], s["ahead_in"], place.other_core())

    def rs_second():
        for p, (first, second) in enumerate(BACK):
            for d in (1, 2, 3):
                net.arrived(rs_slots[p][0][d - 1], s["ra"].at[p, d - 1], place.ring(first, -d))
            here = place.coordinate(first)
            total = (s["g"][p, here] if first == ORDERS[p][2] else s["g"][p, :, here]).astype(F32)
            for d in range(3):
                total += s["ra"][p, d].astype(F32)
            s["s2"][p] = total.astype(BF16)
            mine = place.coordinate(second)
            for d in (1, 2, 3):
                net.start(
                    rs_slots[p][1][d - 1],
                    s["s2"].at[p, (mine + d) % 4],
                    s["rb"].at[p, d - 1],
                    place.ring(second, d),
                )

    def rs_third():
        for p, (_, second) in enumerate(BACK):
            one = ORDERS[p][0]
            for d in (1, 2, 3):
                net.arrived(rs_slots[p][1][d - 1], s["rb"].at[p, d - 1], place.ring(second, -d))
            total = s["s2"][p, place.coordinate(second)].astype(F32)
            for d in range(3):
                total += s["rb"][p, d].astype(F32)
            s["u"][p] = dot_nn(unpack, total.astype(BF16)).astype(BF16).reshape(4, 16, D)
            mine = place.coordinate(one)
            for d in (1, 2, 3):
                net.start(
                    rs_slots[p][2][d - 1],
                    s["u"].at[p, (mine + d) % 4],
                    s["rc"].at[p, d - 1],
                    place.ring(one, d),
                )

    def rs_result():
        for p, (one, _, _) in enumerate(ORDERS):
            for d in (1, 2, 3):
                net.arrived(rs_slots[p][2][d - 1], s["rc"].at[p, d - 1], place.ring(one, -d))
            total = s["u"][p, place.coordinate(one)].astype(F32)
            for d in range(3):
                total += s["rc"][p, d].astype(F32)
            s["f"][pl.ds(16 * p, 16)] = total

    net.arrived(dn2_slot, s["dn2_in"], place.other_core())
    d_normed = s["dn2"][pl.ds(0, 256)] + s["dn2_in"][...].astype(F32)
    middle, inv2 = s["middle"][...], s["inv2"][...]
    unit2 = middle * inv2
    scaled = d_normed * s["gain2"][...]
    inner = jnp.sum(scaled * unit2, axis=1, keepdims=True) * (1.0 / D)
    d_middle = s["dy"][0].astype(F32) + inv2 * (scaled - unit2 * inner)
    s["d_middle"][...] = d_middle
    g_gain2 = jnp.sum(d_normed * unit2, axis=0, keepdims=True)
    d_branch = d_middle.astype(BF16)
    w_out = a2[...].reshape(DP_ROWS, D)
    d_mixed = dot_nt(d_branch, w_out).astype(BF16)
    s["d_mixed"][...] = dot_nt(d_mixed, s["spread"][...]).astype(BF16).reshape(2, 128, D)
    out_sum = SplitSummed(net, place, s["sum_out"])
    rest_sum = Summed(net, place, s["sum_rest"])
    grad = dot_tn(s["mixed_spread"][...], d_branch)
    out_sum.fill(grad[:, 0:512])
    rest_sum.fill(0, grad[:, 512:576])
    out_sum.begin()

    dkv, dkv_in = s["dkv"], s["dkv_in"]
    dkv_slots = [net.new() for _ in range(8)]
    own_slots = [net.new() for _ in range(8)]
    relay_slots = [net.new() for _ in range(8)]
    across_slot = net.new()
    for b in range(2):
        for g in range(3):
            inv = s["inv_sum"][b, g]
            keys = s["kv"][:, b, :, pl.ds(64 * g, 64)].reshape(1024, 64)
            values = s["kv"][:, b, :, pl.ds(192 + 64 * g, 64)].reshape(1024, 64)
            query = heads(s["q"][b], g)
            d_out = (heads(s["d_mixed"][b], g).astype(F32) * inv).astype(BF16)
            inner = jnp.sum(
                d_out.astype(F32) * heads(s["mixed"][b], g).astype(F32), axis=1, keepdims=True
            )
            weight = s["attn"][b, g]
            d_score = (weight.astype(F32) * (dot_nt(d_out, values) - inner)).astype(BF16)
            d_query = dot_nn(d_score, keys) * HEAD_WIDTH**-0.5
            for h in range(3):
                s["dq"][b, :, pl.ds(64 * (3 * g + h), 64)] = d_query[128 * h : 128 * h + 128]
            d_keys = jnp.transpose(dot_tn(query, d_score)).astype(BF16)
            d_values = jnp.transpose(dot_tn(d_out, weight)).astype(BF16)
            s["dkv"][:, b, :, pl.ds(64 * g, 64)] = d_keys.reshape(8, 128, 64)
            s["dkv"][:, b, :, pl.ds(192 + 64 * g, 64)] = d_values.reshape(8, 128, 64)
        if b == 0:
            for k in (2, 4, 6):
                net.start_if(k <= rank, own_slots[k], dkv.at[k, 0], dkv_in.at[k, 0], place.rank(-k))
                other = k - 1 + 2 * place.x_lo
                net.start_if(
                    k <= rank, relay_slots[k], dkv.at[other, 0], s["relay"].at[k // 2 - 1], place.rank(-k)
                )
        else:
            for k in range(1, 8):
                net.start_if(k <= rank, dkv_slots[k], dkv.at[k, 1], dkv_in.at[k, 1], place.rank(-k))
        if b == 0:
            out_sum.over_y()
            rs_second()
    s["relay_sum"][...] = jnp.where(place.x_lo == 1, dkv[1, 0].astype(F32), 0.0)
    for k in (2, 4, 6):

        @pl.when(rank + k <= 7)
        def _(k=k):
            net.arrived(relay_slots[k], s["relay"].at[k // 2 - 1], place.rank(k))
            s["relay_sum"][...] += s["relay"][k // 2 - 1].astype(F32)

    s["across"][...] = s["relay_sum"][...].astype(BF16)
    net.start(across_slot, s["across"], s["across_in"], place.pair())
    net.arrived(out_slot, s["ahead_in"], place.other_core())
    out = s["middle"][...] + s["ahead"][pl.ds(0, 256)] + s["ahead_in"][...].astype(F32)
    for b in range(2):
        out_ref[b] = jnp.transpose(out[128 * b : 128 * b + 128]).astype(BF16)

    cos, sin = s["cos"][...], s["sin"][...]
    lane = iota((256, 128), 1)
    for t in range(5):
        if t < 4:
            tile = s["dq"][:, :, pl.ds(128 * t, 128)].reshape(256, 128)
        else:
            tile = s["dq"][:, :, pl.ds(512, 64)].reshape(256, 64)
            tile = jnp.concatenate([tile, jnp.zeros((256, 64), F32)], axis=1)
        tile = tile * cos - swap_halves(tile) * sin
        s["dqkv"][:, pl.ds(384 + 128 * t, 128)] = tile.astype(BF16)
    n1 = s["n1"][...]
    q_sum = SplitSummed(net, place, s["sum_q"])
    q_sum.fill(dot_tn(n1, s["dqkv"][:, pl.ds(384, 512)]))
    rest_sum.fill(64, dot_tn(n1, s["dqkv"][:, pl.ds(896, 128)])[:, 0:64])
    q_sum.begin()
    rest_sum.begin()
    out_sum.over_group()
    rs_third()
    q_sum.over_y()
    rest_sum.over_group()

    for b in range(2):
        s["dkv_sum"][b] = dkv[0, b].astype(F32)
    for k in range(1, 8):

        @pl.when(rank + k <= 7)
        def _(k=k):
            net.arrived(dkv_slots[k], dkv_in.at[k, 1], place.rank(k))
            s["dkv_sum"][1] += dkv_in[k, 1].astype(F32)
            if k % 2 == 0:
                net.arrived(own_slots[k], dkv_in.at[k, 0], place.rank(k))
                s["dkv_sum"][0] += dkv_in[k, 0].astype(F32)

    net.arrived(across_slot, s["across_in"], place.pair())
    s["dkv_sum"][0] += s["across_in"][...].astype(F32)
    for t in range(3):
        tile = s["dkv_sum"][:, :, pl.ds(128 * t, 128)].reshape(256, 128)
        if t < 2:
            turned = tile * cos - swap_halves(tile) * sin
            tile = jnp.where(lane < 64, turned, tile) if t == 1 else turned
        s["dqkv"][:, pl.ds(128 * t, 128)] = tile.astype(BF16)
    d_pre = s["dqkv"][...]
    d_normed = dot_nt(d_pre, a1[...].reshape(DP_ROWS, 1024))
    unit1 = s["unit1"][...]
    g_gain1 = jnp.sum(d_normed * unit1, axis=0, keepdims=True)
    spread = s["spread"][...]
    g_gain2 = dot_nn(jnp.broadcast_to(g_gain2, (16, D)).astype(BF16), spread)[0:1]
    row = iota((128, DP_ROWS), 0)
    g_gains = jnp.transpose(jnp.where(row == 0, g_gain1, jnp.where(row == 1, g_gain2, 0.0)))
    row, col = iota((DP_ROWS, 128), 0).astype(F32), iota((DP_ROWS, 128), 1).astype(F32)
    within = row - PAD * jnp.floor((row + 0.5) * (1.0 / PAD)) == col
    row, col = iota((BLOCKS, DP_ROWS), 0), iota((BLOCKS, DP_ROWS), 1)
    block = one_hot((col >= row * PAD) & (col < row * PAD + PAD))
    lines = [dot_nn(block, jnp.where(within, g_gains[:, k : k + 1], 0.0).astype(BF16)) for k in range(2)]
    row, col = iota((DP_ROWS, 2 * BLOCKS), 0), iota((DP_ROWS, 2 * BLOCKS), 1)
    put = one_hot(row == (col & 15) * PAD + ROWS + (col >> 4))
    lines = dot_nn(put, jnp.concatenate(lines, axis=0).astype(BF16))
    t_sum = Summed(net, place, s["sum_t"])
    grad = dot_tn(n1, d_pre[:, 0:384])
    t_sum.fill(0, grad[:, 0:128] + lines)
    t_sum.fill(128, grad[:, 128:384])
    t_sum.begin()

    scaled = d_normed * s["gain1"][...]
    inner = jnp.sum(scaled * unit1, axis=1, keepdims=True) * (1.0 / D)
    d_in = s["inv1"][...] * (scaled - unit1 * inner)
    high = d_in.astype(BF16)
    low = (d_in - high.astype(F32)).astype(BF16)
    d_in = s["d_middle"][...] + dot_nt(high, spread) + dot_nt(low, spread)
    t_sum.over_group()
    for b in range(2):
        gx_ref[b] = jnp.transpose(d_in[128 * b : 128 * b + 128]).astype(BF16)
    out_sum.over_pair()
    q_sum.over_group()
    rest_sum.over_ranks()
    rs_result()
    sums = s["f"][...]
    high = sums.astype(BF16)
    low = (sums - high.astype(F32)).astype(BF16)
    row, col = iota((12, PAD), 0), iota((12, PAD), 1)
    for t, ref in enumerate((gg_ref, gu_ref, gd_ref)):
        pick = one_hot(col == ((row >> 2) << 4) + 4 * t + (row & 3))
        ref[...] = dot_nn(pick, high) + dot_nn(pick, low)
    out_sum.back()
    q_sum.over_pair()
    t_sum.over_ranks()
    q_sum.back()
    total = rest_sum.result()
    go_ref[:, pl.ds(512, 64)] = total[0:ROWS, 0:64]
    gq_ref[:, pl.ds(512, 64)] = total[0:ROWS, 64:128]
    out_sum.result(go_ref)
    q_sum.result(gq_ref)
    total = t_sum.result()
    gk_ref[...] = total[0:ROWS, 0:192]
    gv_ref[...] = total[0:ROWS, 192:384]
    gna_ref[...] = total[ROWS : ROWS + 1, 0:ROWS]
    gnm_ref[...] = total[ROWS + 1 : ROWS + 2, 0:ROWS]

    assert net.used <= COPIES, net.used
    net.finish()


def sum_buffers(width):
    return [
        pltpu.VMEM((2, 8, PAD, width), BF16),
        pltpu.VMEM((8, PAD, width), BF16),
        pltpu.VMEM((8, PAD, width), BF16),
        pltpu.VMEM((7, PAD, width), BF16),
        pltpu.VMEM((PAD, width), BF16),
        pltpu.VMEM((7, PAD, width), BF16),
    ]


def split_buffers():
    shapes = [
        (2, 4, 8, PAD, 128),
        (4, 8, PAD, 128),
        (4, 8, PAD, 128),
        (3, 8, PAD, 128),
        (8, PAD, 128),
        (7, PAD, 128),
        (PAD, 128),
        (PAD, 128),
        (4, PAD, 128),
    ]
    return [pltpu.VMEM(shape, BF16) for shape in shapes]


COPIES = 200

SCRATCH = {
    "send": pltpu.SemaphoreType.DMA((COPIES,)),
    "recv": pltpu.SemaphoreType.DMA((COPIES,)),
    "x": pltpu.VMEM((256, D), BF16),
    "tile": pltpu.VMEM((3, 16, D), BF16),
    "first": pltpu.VMEM((3, 4, 16, D), BF16),
    "w": pltpu.VMEM((3, 4, 4, PAD, D), BF16),
    "a1": pltpu.VMEM((BLOCKS, PAD, 1024), BF16),
    "a2": pltpu.VMEM((BLOCKS, PAD, D), BF16),
    "spread": pltpu.VMEM((D, DP_ROWS), BF16),
    "cos": pltpu.VMEM((256, 128), F32),
    "sin": pltpu.VMEM((256, 128), F32),
    "bias": pltpu.VMEM((2, 128, 1024), F32),
    "inv1": pltpu.VMEM((256, 1), F32),
    "unit1": pltpu.VMEM((256, DP_ROWS), F32),
    "gain1": pltpu.VMEM((1, DP_ROWS), F32),
    "gain2": pltpu.VMEM((1, D), F32),
    "n1": pltpu.VMEM((256, DP_ROWS), BF16),
    "q": pltpu.VMEM((2, 128, 640), BF16),
    "kv": pltpu.VMEM((8, 2, 128, 384), BF16),
    "attn": pltpu.VMEM((2, 3, 384, 1024), BF16),
    "inv_sum": pltpu.VMEM((2, 3, 384, 1), F32),
    "mixed": pltpu.VMEM((2, 128, D), BF16),
    "mixed_spread": pltpu.VMEM((256, DP_ROWS), BF16),
    "middle": pltpu.VMEM((256, D), F32),
    "inv2": pltpu.VMEM((256, 1), F32),
    "n2": pltpu.VMEM((2, 256, D), BF16),
    "dy": pltpu.VMEM((2, 256, D), BF16),
    "dn2": pltpu.VMEM((512, D), F32),
    "ahead": pltpu.VMEM((512, D), F32),
    "dn2_out": pltpu.VMEM((256, D), BF16),
    "dn2_in": pltpu.VMEM((256, D), BF16),
    "ahead_out": pltpu.VMEM((256, D), BF16),
    "ahead_in": pltpu.VMEM((256, D), BF16),
    "d_middle": pltpu.VMEM((256, D), F32),
    "d_mixed": pltpu.VMEM((2, 128, D), BF16),
    "dq": pltpu.VMEM((2, 128, D), F32),
    "dkv": pltpu.VMEM((8, 2, 128, 384), BF16),
    "dkv_in": pltpu.VMEM((8, 2, 128, 384), BF16),
    "relay": pltpu.VMEM((3, 128, 384), BF16),
    "relay_sum": pltpu.VMEM((128, 384), F32),
    "across": pltpu.VMEM((128, 384), BF16),
    "across_in": pltpu.VMEM((128, 384), BF16),
    "dkv_sum": pltpu.VMEM((2, 128, 384), F32),
    "dqkv": pltpu.VMEM((256, 1024), BF16),
    "g": pltpu.VMEM((3, 4, 4, PAD, D), BF16),
    "ra": pltpu.VMEM((3, 3, 4, PAD, D), BF16),
    "s2": pltpu.VMEM((3, 4, PAD, D), BF16),
    "rb": pltpu.VMEM((3, 3, PAD, D), BF16),
    "u": pltpu.VMEM((3, 4, 16, D), BF16),
    "rc": pltpu.VMEM((3, 3, 16, D), BF16),
    "f": pltpu.VMEM((PAD, D), F32),
    "sum_out": split_buffers(),
    "sum_q": split_buffers(),
    "sum_rest": sum_buffers(128),
    "sum_t": sum_buffers(384),
}


def hand_over(*refs):
    count = len(refs) // 2
    for a, b in zip(refs[:count], refs[count:]):
        b[...] = a[...]


def local(
    inputs, segment_ids, norm_attn, w_query, w_key, w_value, w_out, norm_mlp, w_gate, w_up, w_down, cotangent,
):
    half = HEAD_WIDTH // 2
    freq = np.float32(ROPE_BASE) ** (-(np.float32(2.0) * np.arange(half, dtype=np.float32)) / HEAD_WIDTH)
    freq = jnp.asarray(np.tile(freq.astype(np.float32), 4)[None, :])
    shapes = [
        ((2, D, 128), BF16),
        ((2, D, 128), BF16),
        ((1, ROWS), F32),
        ((ROWS, 576), F32),
        ((ROWS, 192), F32),
        ((ROWS, 192), F32),
        ((ROWS, D), F32),
        ((1, ROWS), F32),
        ((12, D), F32),
        ((12, D), F32),
        ((12, D), F32),
    ]
    shapes = [jax.ShapeDtypeStruct(shape, dtype) for shape, dtype in shapes]
    count = len(shapes)
    outs = pl.pallas_call(
        kernel,
        out_shape=shapes,
        in_specs=[pl.BlockSpec(memory_space=pltpu.VMEM)] * 13,
        out_specs=[pl.BlockSpec(memory_space=pltpu.VMEM)] * count,
        scratch_shapes=[SCRATCH],
        compiler_params=pltpu.CompilerParams(
            collective_id=0, has_side_effects=True, vmem_limit_bytes=60 * 2**20
        ),
        name="layer",
    )(
        jnp.transpose(inputs, (0, 2, 1)), segment_ids, norm_attn[None, :], w_query, w_key, w_value, w_out,
        norm_mlp[None, :], w_gate.T, w_up.T, w_down, jnp.transpose(cotangent, (0, 2, 1)), freq,
    )
    outs = pl.pallas_call(
        hand_over,
        out_shape=shapes,
        in_specs=[pl.BlockSpec(memory_space=pltpu.VMEM)] * count,
        out_specs=[pl.BlockSpec(memory_space=pltpu.VMEM)] * count,
        name="hand_over",
    )(*outs)
    outs = list(outs)
    for k in (0, 1):
        outs[k] = jnp.transpose(outs[k], (0, 2, 1))
    for k in (2, 7):
        outs[k] = outs[k].reshape(ROWS)
    for k in (8, 9):
        outs[k] = outs[k].T
    return tuple(outs)


def solution(mesh):
    rows, both = P("dp", None), ("dp", "seq")
    tokens = P("dp", "seq", None)
    weights = (P("dp"), rows, rows, rows, rows, P("dp"), P(None, both), P(None, both), P(both, None))
    return jax.shard_map(
        local,
        mesh=mesh,
        in_specs=(tokens, P("dp", None), *weights, tokens),
        out_specs=(tokens, tokens, *weights),
        check_vma=False,
    )
```

```python
import functools
import types

import jax
import jax.numpy as jnp
import numpy as np
from jax import lax
from jax.experimental import pallas as pl
from jax.experimental.pallas import tpu as pltpu
from jax.sharding import PartitionSpec as P

MESH = pl.DeviceIdType.MESH
F32 = jnp.float32
BF16 = jnp.bfloat16

D = 576
FF = 1536
QUERY_HEADS = 9
KV_HEADS = 3
HEAD_WIDTH = 64
ROPE_BASE = 100000.0
NORM_EPS = 1e-05
MASKED = -1e30

ROWS = 36
PAD = 48
BLOCKS = 16
DP_ROWS = BLOCKS * PAD
ORDERS = (("x", "y", "z"), ("y", "z", "x"), ("z", "x", "y"))
BACK = (("z", "y"), ("z", "x"), ("x", "y"))


def dot_nn(a, b):
    return lax.dot_general(a, b, (((1,), (0,)), ((), ())), preferred_element_type=F32)


def dot_nt(a, b):
    return lax.dot_general(a, b, (((1,), (1,)), ((), ())), preferred_element_type=F32)


def dot_tn(a, b):
    return lax.dot_general(a, b, (((0,), (0,)), ((), ())), preferred_element_type=F32)


def iota(shape, dim):
    return lax.broadcasted_iota(jnp.int32, shape, dim)


def one_hot(cond):
    return jnp.where(cond, 1.0, 0.0).astype(BF16)


class Place:
    def __init__(self):
        self.dp = lax.axis_index("dp")
        self.seq = lax.axis_index("seq")
        self.z = self.dp // 4
        self.x_hi = (self.dp // 2) % 2
        self.core = self.dp % 2
        self.y = self.seq // 2
        self.x_lo = self.seq % 2
        self.x = 2 * self.x_hi + self.x_lo

    def at(self, x, y, z, core):
        return (z * 4 + (x // 2) * 2 + core, y * 2 + x % 2)

    def coordinate(self, axis):
        return {"x": self.x, "y": self.y, "z": self.z}[axis]

    def ring(self, axis, step):
        here = {"x": self.x, "y": self.y, "z": self.z}
        here[axis] = (here[axis] + step + 4) % 4
        return self.at(here["x"], here["y"], here["z"], self.core)

    def other_core(self):
        return (self.dp + 1 - 2 * self.core, self.seq)

    def group(self, dz, dx):
        z = (self.z + dz + 4) % 4
        x = 3 - self.x if dx else self.x
        return self.at(x, self.y, z, self.core), z * 2 + x // 2

    def pair(self):
        return self.at(self.x + 1 - 2 * self.x_lo, self.y, self.z, self.core)

    def rank(self, step):
        return (self.dp, (self.seq + step + 8) % 8)


class Net:
    def __init__(self, send, recv):
        self.send, self.recv, self.used = send, recv, 0
        self.unsent, self.maybe_unsent = [], []

    def new(self):
        self.used += 1
        return self.used - 1

    def copy(self, slot, src, dst, device):
        return pltpu.make_async_remote_copy(
            src_ref=src,
            dst_ref=dst,
            send_sem=self.send.at[slot],
            recv_sem=self.recv.at[slot],
            device_id=device,
            device_id_type=MESH,
        )

    def start(self, slot, src, dst, device):
        copy = self.copy(slot, src, dst, device)
        copy.start()
        self.unsent.append(copy)

    def arrived(self, slot, dst, device):
        self.copy(slot, dst, dst, device).wait_recv()

    def start_if(self, wanted, slot, src, dst, device):
        copy = self.copy(slot, src, dst, device)
        pl.when(wanted)(copy.start)
        self.maybe_unsent.append((wanted, copy))

    def arrived_if(self, wanted, slot, dst, device):
        pl.when(wanted)(functools.partial(self.arrived, slot, dst, device))

    def finish(self):
        for copy in self.unsent:
            copy.wait_send()
        for wanted, copy in self.maybe_unsent:
            pl.when(wanted)(copy.wait_send)


GROUP_STEPS = [(dz, dx) for dz in range(4) for dx in range(2) if (dz, dx) != (0, 0)]


class Summed:
    def __init__(self, net, place, refs):
        self.net, self.place = net, place
        (
            self.mine, self.from_core, self.chip, self.from_group, self.one, self.from_y, self.two, self.from_pair,
        ) = refs
        self.core_slot, self.pair_slot = net.new(), net.new()
        self.group_slots = [net.new() for _ in GROUP_STEPS]
        self.y_slots = [net.new() for _ in range(3)]

    def begin(self, value):
        place = self.place
        value = value.astype(BF16).reshape(8, 2, PAD, value.shape[1])
        for c in range(2):
            self.mine[c] = value[:, c]
        self.net.start(
            self.core_slot, self.mine.at[1 - place.core], self.from_core, place.other_core()
        )

    def over_group(self):
        place, net = self.place, self.net
        net.arrived(self.core_slot, self.from_core, place.other_core())
        self.chip[...] = (
            self.mine[place.core].astype(F32) + self.from_core[...].astype(F32)
        ).astype(BF16)
        for k, (dz, dx) in enumerate(GROUP_STEPS):
            device, index = place.group(dz, dx)
            net.start(self.group_slots[k], self.chip.at[index], self.from_group.at[k], device)

    def over_y(self):
        place, net = self.place, self.net
        for k, (dz, dx) in enumerate(GROUP_STEPS):
            device, _ = place.group(-dz, dx)
            net.arrived(self.group_slots[k], self.from_group.at[k], device)
        total = self.chip[place.z * 2 + place.x_hi].astype(F32)
        for k in range(7):
            total += self.from_group[k].astype(F32)
        self.one[...] = total.astype(BF16)
        for d in (1, 2, 3):
            net.start(self.y_slots[d - 1], self.one, self.from_y.at[d - 1], place.ring("y", d))

    def over_pair(self):
        place, net = self.place, self.net
        for d in (1, 2, 3):
            net.arrived(self.y_slots[d - 1], self.from_y.at[d - 1], place.ring("y", -d))
        total = self.one[...].astype(F32)
        for d in range(3):
            total += self.from_y[d].astype(F32)
        self.two[...] = total.astype(BF16)
        net.start(self.pair_slot, self.two, self.from_pair, place.pair())

    def result(self):
        self.net.arrived(self.pair_slot, self.from_pair, self.place.pair())
        return self.two[...].astype(F32) + self.from_pair[...].astype(F32)


class SplitSummed:
    def __init__(self, net, place, refs):
        self.net, self.place = net, place
        (
            self.mine, self.from_core, self.chip, self.from_y, self.part, self.from_group, self.one, self.from_pair,
            self.whole,
        ) = refs
        self.core_slot, self.pair_slot = net.new(), net.new()
        self.y_slots = [net.new() for _ in range(3)]
        self.group_slots = [net.new() for _ in GROUP_STEPS]
        self.back_slots = [net.new() for _ in range(3)]

    def fill(self, value):
        value = value.astype(BF16)
        for t in range(4):
            tile = value[:, 128 * t : 128 * t + 128].reshape(8, 2, PAD, 128)
            for c in range(2):
                self.mine[c, t] = tile[:, c]

    def begin(self):
        place = self.place
        self.net.start(
            self.core_slot, self.mine.at[1 - place.core], self.from_core, place.other_core()
        )

    def over_y(self):
        place, net = self.place, self.net
        net.arrived(self.core_slot, self.from_core, place.other_core())
        self.chip[...] = (
            self.mine[place.core].astype(F32) + self.from_core[...].astype(F32)
        ).astype(BF16)
        for d in (1, 2, 3):
            net.start(
                self.y_slots[d - 1],
                self.chip.at[(place.y + d) % 4],
                self.from_y.at[d - 1],
                place.ring("y", d),
            )

    def over_group(self):
        place, net = self.place, self.net
        for d in (1, 2, 3):
            net.arrived(self.y_slots[d - 1], self.from_y.at[d - 1], place.ring("y", -d))
        total = self.chip[place.y].astype(F32)
        for d in range(3):
            total += self.from_y[d].astype(F32)
        self.part[...] = total.astype(BF16)
        for k, (dz, dx) in enumerate(GROUP_STEPS):
            device, index = place.group(dz, dx)
            net.start(self.group_slots[k], self.part.at[index], self.from_group.at[k], device)

    def over_pair(self):
        place, net = self.place, self.net
        for k, (dz, dx) in enumerate(GROUP_STEPS):
            device, _ = place.group(-dz, dx)
            net.arrived(self.group_slots[k], self.from_group.at[k], device)
        total = self.part[place.z * 2 + place.x_hi].astype(F32)
        for k in range(7):
            total += self.from_group[k].astype(F32)
        self.one[...] = total.astype(BF16)
        net.start(self.pair_slot, self.one, self.from_pair, place.pair())

    def back(self):
        place, net = self.place, self.net
        net.arrived(self.pair_slot, self.from_pair, place.pair())
        total = self.one[...].astype(F32) + self.from_pair[...].astype(F32)
        self.whole[place.y] = total.astype(BF16)
        for d in (1, 2, 3):
            tile = self.whole.at[place.y]
            net.start(self.back_slots[d - 1], tile, tile, place.ring("y", d))

    def result(self, ref):
        place, net = self.place, self.net
        for d in (1, 2, 3):
            net.arrived(
                self.back_slots[d - 1], self.whole.at[(place.y + 4 - d) % 4], place.ring("y", -d)
            )
        for t in range(4):
            ref[:, pl.ds(128 * t, 128)] = self.whole[t, pl.ds(0, ROWS)].astype(F32)


class Gathered:
    def __init__(self, net, place, whole):
        self.net, self.place, self.whole = net, place, whole
        self.group_slots = [net.new() for _ in GROUP_STEPS]
        self.core_slots = [net.new() for _ in range(8)]

    def begin(self):
        place, net = self.place, self.net
        block = self.whole.at[place.dp]
        for k, (dz, dx) in enumerate(GROUP_STEPS):
            net.start(self.group_slots[k], block, block, place.group(dz, dx)[0])
        net.start(self.core_slots[7], block, block, place.other_core())

    def pass_on(self):
        place, net = self.place, self.net
        for k, (dz, dx) in enumerate(GROUP_STEPS):
            device, index = place.group(-dz, dx)
            block = self.whole.at[index * 2 + place.core]
            net.arrived(self.group_slots[k], block, device)
            net.start(self.core_slots[k], block, block, place.other_core())

    def finish(self):
        place, net = self.place, self.net
        for k, (dz, dx) in enumerate(GROUP_STEPS):
            _, index = place.group(-dz, dx)
            block = self.whole.at[index * 2 + 1 - place.core]
            net.arrived(self.core_slots[k], block, place.other_core())
        net.arrived(self.core_slots[7], self.whole.at[place.other_core()[0]], place.other_core())


def swap_halves(tile):
    first = (iota(tile.shape, 1) & 32) == 0
    return jnp.where(first, pltpu.roll(tile, 96, 1), pltpu.roll(tile, 32, 1))


def kernel(
    x_ref, dy_ref, seg_ref, na_ref, wq_ref, wk_ref, wv_ref, wo_ref, nm_ref, wg_ref, wu_ref, wd_ref, lane_freq_ref,
    row_freq_ref,
    out_ref, gx_ref, gna_ref, gq_ref, gk_ref, gv_ref, go_ref, gnm_ref, gg_ref, gu_ref, gd_ref,
    s,
):
    s = types.SimpleNamespace(**s)
    place = Place()
    net = Net(s.send, s.recv)
    rank = place.seq
    apart = place.x_lo == 0
    xs = s.xs

    barrier = pltpu.get_barrier_semaphore()
    peers = [place.ring(axis, step) for axis in "xyz" for step in (1, 2, 3)]
    peers += [place.other_core()]
    peers += [place.group(dz, 1)[0] for dz in (1, 2, 3)]
    flipped = place.x + 1 - 2 * place.x_lo
    peers += [place.at(flipped, (place.y + dy) % 4, place.z, place.core) for dy in (1, 2, 3)]
    for peer in peers:
        pl.semaphore_signal(barrier, inc=1, device_id=peer, device_id_type=MESH)
    x_copy = pltpu.make_async_copy(x_ref, xs.at[0], s.local.at[0])
    dy_copy = pltpu.make_async_copy(dy_ref, s.dy_t, s.local.at[1])
    x_copy.start()
    dy_copy.start()

    a_kv, a_q, a_out = s.a_kv, s.a_q, s.a_out
    down = one_hot(iota((PAD, ROWS), 0) == iota((PAD, ROWS), 1))
    keys, values = dot_nn(down, wk_ref[...]), dot_nn(down, wv_ref[...])
    widen = one_hot(iota((ROWS, 128), 0) == iota((ROWS, 128), 1))
    row = iota((PAD, 128), 0)
    for g in range(3):
        tile = jnp.concatenate([keys[:, 64 * g : 64 * g + 64], values[:, 64 * g : 64 * g + 64]], axis=1)
        if g == 0:
            for k, ref in enumerate((na_ref, nm_ref)):
                line = dot_nn(jnp.broadcast_to(ref[...], (16, ROWS)), widen)[0:1]
                tile = tile + jnp.where(row == ROWS + k, line, 0.0)
        a_kv[place.dp, :, pl.ds(128 * g, 128)] = tile.astype(BF16)
    a_q[place.dp] = dot_nn(down, wq_ref[...]).astype(BF16)
    a_out[place.dp] = dot_nn(down, wo_ref[...]).astype(BF16)

    row, col = iota((16, 12), 0), iota((16, 12), 1)
    for p in range(3):
        tile = jnp.zeros((16, D), F32)
        for t, ref in enumerate((wg_ref, wu_ref, wd_ref)):
            pick = one_hot(((row >> 2) == t) & (col == 4 * p + (row & 3)))
            tile += dot_nn(pick, ref[...])
        s.tile[p] = tile.astype(BF16)

    kv_weights, q_weights, out_weights = (Gathered(net, place, a) for a in (a_kv, a_q, a_out))
    ff_slots = [[[net.new() for _ in range(3)] for _ in range(3)] for _ in range(3)]
    dy_slot, n2_slot, out_slot, dn2_slot = (net.new() for _ in range(4))
    x_slots = [net.new() for _ in range(8)]
    column_slots = [net.new() for _ in range(8)]
    across_slots = [net.new() for _ in range(8)]

    x_copy.wait()
    pl.semaphore_wait(barrier, len(peers))

    for p, (one, _, _) in enumerate(ORDERS):
        mine = place.coordinate(one)
        s.first[p, mine] = s.tile[p]
        for d in (1, 2, 3):
            net.start(
                ff_slots[p][0][d - 1], s.tile.at[p], s.first.at[p, mine], place.ring(one, d)
            )
    kv_weights.begin()
    for k in (2, 4, 6):
        net.start_if(rank + k <= 7, column_slots[k], xs.at[0, 1], xs.at[k, 1], place.rank(k))
    net.start_if(apart, across_slots[1], xs.at[0, 1], xs.at[1, 1], place.pair())
    for k in range(1, 8):
        net.start_if(rank + k <= 7, x_slots[k], xs.at[0, 0], xs.at[k, 0], place.rank(k))
    q_weights.begin()
    out_weights.begin()
    dy_copy.wait()
    for b in range(2):
        s.x[pl.ds(128 * b, 128)] = jnp.transpose(xs[0, b].astype(F32)).astype(BF16)
        s.dy[0, pl.ds(128 * b, 128)] = jnp.transpose(s.dy_t[b].astype(F32)).astype(BF16)
    net.start(dy_slot, s.dy.at[0], s.dy.at[1], place.other_core())

    row, col = iota((PAD, 64), 0), iota((PAD, 64), 1)
    pack = one_hot(col == (((row >> 2) & 3) << 4) + ((row >> 4) << 2) + (row & 3))
    row, col = iota((64, PAD), 0), iota((64, PAD), 1)
    unpack = one_hot(row == (((col >> 2) & 3) << 4) + ((col >> 4) << 2) + (col & 3))

    def ff_second():
        for p, (one, two, three) in enumerate(ORDERS):
            mine = place.coordinate(one)
            for d in (1, 2, 3):
                net.arrived(
                    ff_slots[p][0][d - 1], s.first.at[p, (mine + 4 - d) % 4], place.ring(one, -d)
                )
            block = s.w.at[p, place.coordinate(three), place.coordinate(two)]
            block[...] = dot_nn(pack, s.first[p].reshape(64, D)).astype(BF16)
            for d in (1, 2, 3):
                net.start(ff_slots[p][1][d - 1], block, block, place.ring(two, d))

    def ff_third(p):
        _, two, three = ORDERS[p]
        mine, last = place.coordinate(two), place.coordinate(three)
        for d in (1, 2, 3):
            net.arrived(
                ff_slots[p][1][d - 1], s.w.at[p, last, (mine + 4 - d) % 4], place.ring(two, -d)
            )
        block = s.w.at[p, last]
        for d in (1, 2, 3):
            net.start(ff_slots[p][2][d - 1], block, block, place.ring(three, d))

    def ff_have(p):
        three = ORDERS[p][2]
        last = place.coordinate(three)
        for d in (1, 2, 3):
            net.arrived(
                ff_slots[p][2][d - 1], s.w.at[p, (last + 4 - d) % 4], place.ring(three, -d)
            )

    for k in range(1, 8):

        @pl.when(k > rank)
        def _(k=k):
            xs[k] = jnp.zeros((2, D, 128), BF16)

    row = iota((D, DP_ROWS), 0).astype(F32)
    col = iota((D, DP_ROWS), 1).astype(F32)
    s.spread[...] = one_hot(col - row == 12.0 * jnp.floor((row + 0.5) * (1.0 / ROWS)))
    def tables(b):
        lane = iota((128, 128), 1)
        own = seg_ref[pl.ds(b, 1), pl.ds(pl.multiple_of(rank * 128, 128), 128)].astype(F32)
        own = jnp.transpose(jnp.broadcast_to(own, (128, 128)))
        earlier = jnp.zeros((128, 128), F32)
        for c in range(8):
            part = seg_ref[pl.ds(b, 1), pl.ds(128 * c, 128)].astype(F32)
            earlier += jnp.where(part < own, 1.0, 0.0)
            s.seg[pl.ds(128 * c, 128)] = jnp.transpose(jnp.broadcast_to(part, (128, 128)))
        begin = jnp.sum(earlier, axis=1, keepdims=True)
        here = (iota((128, 1), 0) + rank * 128).astype(F32)
        angle = (here - begin) * lane_freq_ref[...]
        s.cos[pl.ds(128 * b, 128)] = jnp.cos(angle)
        sine = jnp.sin(angle)
        s.sin[pl.ds(128 * b, 128)] = jnp.where((lane & 32) == 0, -sine, sine)
        for k in range(8):
            key = (lane + 128 * (rank - k)).astype(F32)
            s.bias[b, :, pl.ds(128 * k, 128)] = jnp.where(
                (key >= begin) & (key <= here), 0.0, MASKED
            )
            first = pl.multiple_of(jnp.maximum(rank - k, 0) * 128, 128)
            part = seg_ref[pl.ds(b, 1), pl.ds(first, 128)].astype(F32)
            begins = jnp.sum(jnp.where(s.seg[...] < part, 1.0, 0.0), axis=0, keepdims=True)
            angle = ((iota((1, 128), 1) + first).astype(F32) - begins) * row_freq_ref[...]
            s.cos_t[b, :, pl.ds(128 * k, 128)] = jnp.cos(angle)
            s.sin_t[b, :, pl.ds(128 * k, 128)] = jnp.sin(angle)

    x32 = s.x[...].astype(F32)
    s.inv1[...] = lax.rsqrt(jnp.sum(x32 * x32, axis=1, keepdims=True) * (1.0 / D) + NORM_EPS)

    tables(0)
    tables(1)
    ff_second()
    kv_weights.pass_on()
    for k in (2, 6, 4):
        net.arrived_if(k <= rank, column_slots[k], xs.at[k, 1], place.rank(-k))
        here = k <= rank
        net.start_if(here & apart, across_slots[k + 1], xs.at[k, 1], xs.at[k + 1, 1], place.pair())
        net.start_if(
            here & jnp.logical_not(apart), across_slots[k - 1], xs.at[k, 1], xs.at[k - 1, 1], place.pair()
        )
    q_weights.pass_on()
    for p in range(3):
        ff_third(p)
    kv_weights.finish()

    spread = s.spread[...]
    row, col = iota((BLOCKS, DP_ROWS), 0), iota((BLOCKS, DP_ROWS), 1)
    a_kv_tile = a_kv[:, :, pl.ds(0, 128)].reshape(DP_ROWS, 128)
    line1, line2 = (
        dot_nn(one_hot(col == row * PAD + ROWS + k), a_kv_tile).astype(BF16) for k in range(2)
    )
    row, col = iota((D, 128), 0).astype(F32), iota((D, 128), 1).astype(F32)
    within = one_hot(row - ROWS * jnp.floor((row + 0.5) * (1.0 / ROWS)) == col)
    row, col = iota((BLOCKS, D), 0), iota((BLOCKS, D), 1)
    block = (col >= row * ROWS) & (col < row * ROWS + ROWS)
    gain1, gain2 = (
        jnp.sum(jnp.where(block, dot_nt(line, within), 0.0), axis=0, keepdims=True) for line in (line1, line2)
    )
    s.gain1[...] = gain1
    s.gain2[...] = gain2
    row, col = iota((D, BLOCKS), 0), iota((D, BLOCKS), 1)
    block_t = (row >= col * ROWS) & (row < col * ROWS + ROWS)
    gain1_t = jnp.sum(jnp.where(block_t, dot_nt(within, line1), 0.0), axis=1, keepdims=True)
    s.w_kv[...] = dot_nn(spread, a_kv[...].reshape(DP_ROWS, 384)).astype(BF16)
    q_weights.finish()
    w_q = dot_nn(spread, a_q[...].reshape(DP_ROWS, D))
    for g in range(3):
        part = [w_q[:, 192 * g : 192 * g + 192], jnp.zeros((D, 64), F32)]
        s.w_q[g] = jnp.concatenate(part, axis=1).astype(BF16)

    n1 = s.x[...].astype(F32) * s.inv1[...] * gain1
    n1 = n1.astype(BF16)
    for g in range(3):
        pre = dot_nn(n1, s.w_q[g])
        for t in range(2):
            tile = pre[:, 128 * t : 128 * t + 128]
            tile = tile * s.cos[...] + swap_halves(tile) * s.sin[...]
            tile = (tile * HEAD_WIDTH**-0.5).astype(BF16).reshape(2, 128, 128)
            s.q[g, :, :, pl.ds(128 * t, 128)] = tile

    def heads(value, first):
        return jnp.concatenate(
            [value[:, 64 * h : 64 * h + 64] for h in range(first, first + 3)], axis=0
        )

    def turned(value, b, back):
        cos, sin = s.cos_t[b], s.sin_t[b]
        one, two = value[0:32], value[32:64]
        if back:
            return one * cos + two * sin, two * cos - one * sin
        return one * cos - two * sin, two * cos + one * sin

    for b in range(2):
        for k in range(1, 8):
            if b == 0:
                net.arrived_if(k <= rank, x_slots[k], xs.at[k, 0], place.rank(-k))
            elif k % 2 == 1:
                net.arrived_if(k <= rank, across_slots[k], xs.at[k, 1], place.pair())
        for k in range(8):
            part = xs[k, b].astype(F32)
            inv = lax.rsqrt(jnp.sum(part * part, axis=0, keepdims=True) * (1.0 / D) + NORM_EPS)
            s.n1[b, :, pl.ds(128 * k, 128)] = (part * inv * gain1_t).astype(BF16)
        both = dot_tn(s.w_kv[...], s.n1[b])
        for g in range(3):
            one, two = turned(both[128 * g : 128 * g + 64], b, False)
            s.k[b, g, pl.ds(0, 32)] = one.astype(BF16)
            s.k[b, g, pl.ds(32, 32)] = two.astype(BF16)
            s.v[b, g] = both[128 * g + 64 : 128 * g + 128].astype(BF16)

        bias = s.bias[b]
        for g in range(3):
            query = heads(s.q[g, b], 0)
            score = dot_nn(query, s.k[b, g])
            score = (score.reshape(3, 128, 1024) + bias[None]).reshape(384, 1024)
            top = jnp.max(score, axis=1, keepdims=True)
            score = jnp.exp(score - top)
            inv = 1.0 / jnp.sum(score, axis=1, keepdims=True)
            weight = score.astype(BF16)
            s.attn[b, g] = weight
            s.inv_sum[b, g] = inv
            mixed = (dot_nt(weight, s.v[b, g]) * inv).astype(BF16)
            for h in range(3):
                s.mixed[b, :, pl.ds(64 * (3 * g + h), 64)] = mixed[128 * h : 128 * h + 128]
        if b == 0:
            out_weights.pass_on()

    out_weights.finish()
    w_out = a_out[...].reshape(DP_ROWS, D)
    s.mixed_spread[...] = dot_nn(s.mixed[...].reshape(256, D), s.spread[...]).astype(BF16)
    middle = s.x[...].astype(F32) + dot_nn(s.mixed_spread[...], w_out)
    s.middle[...] = middle
    inv2 = lax.rsqrt(jnp.sum(middle * middle, axis=1, keepdims=True) * (1.0 / D) + NORM_EPS)
    s.inv2[...] = inv2
    s.n2[0] = (middle * inv2 * s.gain2[...]).astype(BF16)
    net.start(n2_slot, s.n2.at[0], s.n2.at[1], place.other_core())
    net.arrived(dy_slot, s.dy.at[1], place.other_core())
    net.arrived(n2_slot, s.n2.at[1], place.other_core())

    rs_slots = [[[net.new() for _ in range(3)] for _ in range(3)] for _ in range(3)]
    normed, upper = s.n2[...].reshape(512, D), s.dy[...].reshape(512, D)
    for p in (0, 2, 1):
        ff_have(p)
        w_gate, w_up, w_down = (
            s.w[p, :, :, pl.ds(16 * t, 16), :].reshape(256, D) for t in range(3)
        )
        gate = dot_nt(normed, w_gate)
        up = dot_nt(normed, w_up)
        d_act = dot_nt(upper, w_down)
        sigmoid = 1.0 / (1.0 + jnp.exp(-gate))
        silu = gate * sigmoid
        act = (silu * up).astype(BF16)
        d_gate = (d_act * up * sigmoid * (1.0 + gate * (1.0 - sigmoid))).astype(BF16)
        d_up = (d_act * silu).astype(BF16)
        back = dot_nn(d_gate, w_gate) + dot_nn(d_up, w_up)
        ahead = dot_nn(act, w_down)
        if p == 0:
            s.dn2[...] = back
            s.ahead[...] = ahead
        else:
            s.dn2[...] += back
            s.ahead[...] += ahead
        for t, (left, right) in enumerate(((d_gate, normed), (d_up, normed), (act, upper))):
            s.g[p, :, :, pl.ds(16 * t, 16), :] = (
                dot_tn(left, right).astype(BF16).reshape(4, 4, 16, D)
            )
        first = BACK[p][0]
        mine = place.coordinate(first)
        for d in (1, 2, 3):
            there = (mine + d) % 4
            net.start(
                rs_slots[p][0][d - 1],
                s.g.at[p, there] if first == ORDERS[p][2] else s.g.at[p, :, there],
                s.ra.at[p, d - 1],
                place.ring(first, d),
            )
    s.dn2_out[...] = s.dn2[pl.ds(256, 256)].astype(BF16)
    net.start(dn2_slot, s.dn2_out, s.dn2_in, place.other_core())
    s.ahead_out[...] = s.ahead[pl.ds(256, 256)].astype(BF16)
    net.start(out_slot, s.ahead_out, s.ahead_in, place.other_core())

    def rs_second(p):
        first, second = BACK[p]
        for d in (1, 2, 3):
            net.arrived(rs_slots[p][0][d - 1], s.ra.at[p, d - 1], place.ring(first, -d))
        here = place.coordinate(first)
        total = (s.g[p, here] if first == ORDERS[p][2] else s.g[p, :, here]).astype(F32)
        for d in range(3):
            total += s.ra[p, d].astype(F32)
        s.s2[p] = total.astype(BF16)
        mine = place.coordinate(second)
        for d in (1, 2, 3):
            net.start(
                rs_slots[p][1][d - 1],
                s.s2.at[p, (mine + d) % 4],
                s.rb.at[p, d - 1],
                place.ring(second, d),
            )

    def rs_third(p):
        one, second = ORDERS[p][0], BACK[p][1]
        for d in (1, 2, 3):
            net.arrived(rs_slots[p][1][d - 1], s.rb.at[p, d - 1], place.ring(second, -d))
        total = s.s2[p, place.coordinate(second)].astype(F32)
        for d in range(3):
            total += s.rb[p, d].astype(F32)
        s.u[p] = dot_nn(unpack, total.astype(BF16)).astype(BF16).reshape(4, 16, D)
        mine = place.coordinate(one)
        for d in (1, 2, 3):
            net.start(
                rs_slots[p][2][d - 1],
                s.u.at[p, (mine + d) % 4],
                s.rc.at[p, d - 1],
                place.ring(one, d),
            )

    def rs_result():
        for p, (one, _, _) in enumerate(ORDERS):
            for d in (1, 2, 3):
                net.arrived(rs_slots[p][2][d - 1], s.rc.at[p, d - 1], place.ring(one, -d))
            total = s.u[p, place.coordinate(one)].astype(F32)
            for d in range(3):
                total += s.rc[p, d].astype(F32)
            s.f[pl.ds(16 * p, 16)] = total

    net.arrived(dn2_slot, s.dn2_in, place.other_core())
    d_normed = s.dn2[pl.ds(0, 256)] + s.dn2_in[...].astype(F32)
    middle, inv2 = s.middle[...], s.inv2[...]
    unit2 = middle * inv2
    scaled = d_normed * s.gain2[...]
    inner = jnp.sum(scaled * unit2, axis=1, keepdims=True) * (1.0 / D)
    d_middle = s.dy[0].astype(F32) + inv2 * (scaled - unit2 * inner)
    s.d_middle[...] = d_middle
    g_gain2 = jnp.sum(d_normed * unit2, axis=0, keepdims=True)
    d_branch = d_middle.astype(BF16)
    w_out = a_out[...].reshape(DP_ROWS, D)
    d_mixed = dot_nt(d_branch, w_out).astype(BF16)
    s.d_mixed[...] = dot_nt(d_mixed, s.spread[...]).astype(BF16).reshape(2, 128, D)
    out_sum = SplitSummed(net, place, s.sum_out)
    grad = dot_tn(s.mixed_spread[...], d_branch)
    out_sum.fill(grad[:, 0:512])
    out_sum.begin()
    out_tail = grad[:, 512:576]
    lines = dot_nn(jnp.where(block, g_gain2, 0.0).astype(BF16), within).astype(BF16)
    row, col = iota((DP_ROWS, BLOCKS), 0), iota((DP_ROWS, BLOCKS), 1)
    lines = dot_nn(one_hot(row == col * PAD + ROWS), lines)

    dkv, dkv_in = s.dkv, s.dkv_in
    dkv_slots = [[net.new() for _ in range(8)] for _ in range(3)]
    own_slots = [[net.new() for _ in range(8)] for _ in range(3)]
    relay_slots = [[net.new() for _ in range(8)] for _ in range(3)]
    cross_slots = [net.new() for _ in range(3)]
    sums = [Summed(net, place, s.sums[g]) for g in range(3)]

    def relay(g):
        total = s.relay_sum
        total[...] = jnp.where(place.x_lo == 1, dkv[0, g, 1].astype(F32), 0.0)
        for k in (2, 4, 6):

            @pl.when(rank + k <= 7)
            def _(k=k):
                net.arrived(relay_slots[g][k], s.relay.at[g, k // 2 - 1], place.rank(k))
                total[...] += s.relay[g, k // 2 - 1].astype(F32)

        s.cross[g] = total[...].astype(BF16)
        net.start(cross_slots[g], s.cross.at[g], s.cross_in.at[g], place.pair())

    for g in range(3):
        grad = jnp.zeros((D, 128), F32)
        for b in range(2):
            inv = s.inv_sum[b, g]
            query = heads(s.q[g, b], 0)
            d_out = (heads(s.d_mixed[b], 3 * g).astype(F32) * inv).astype(BF16)
            inner = jnp.sum(
                d_out.astype(F32) * heads(s.mixed[b], 3 * g).astype(F32), axis=1, keepdims=True
            )
            weight = s.attn[b, g]
            d_score = (weight.astype(F32) * (dot_nn(d_out, s.v[b, g]) - inner)).astype(BF16)
            d_query = dot_nt(d_score, s.k[b, g]) * HEAD_WIDTH**-0.5
            for h in range(3):
                s.dq[pl.ds(128 * b, 128), pl.ds(64 * h, 64)] = d_query[128 * h : 128 * h + 128]
            one, two = turned(dot_tn(query, d_score), b, True)
            both = jnp.concatenate([one, two, dot_tn(d_out, weight)], axis=0).astype(BF16)
            for k in range(8):
                dkv[b, g, k] = both[:, 128 * k : 128 * k + 128]
            if b == 0:
                for k in (2, 4, 6):
                    net.start_if(
                        k <= rank, own_slots[g][k], dkv.at[0, g, k], dkv_in.at[0, g, k], place.rank(-k)
                    )
                    other = k - 1 + 2 * place.x_lo
                    net.start_if(
                        k <= rank,
                        relay_slots[g][k],
                        dkv.at[0, g, other],
                        s.relay.at[g, k // 2 - 1],
                        place.rank(-k),
                    )
            else:
                for k in range(1, 8):
                    net.start_if(
                        k <= rank, dkv_slots[g][k], dkv.at[1, g, k], dkv_in.at[1, g, k], place.rank(-k)
                    )
            grad += dot_nt(s.n1[b], both)
        d_queries = []
        for t in range(2):
            if t == 0:
                tile = s.dq[:, pl.ds(0, 128)]
            else:
                tile = jnp.concatenate([s.dq[:, pl.ds(128, 64)], jnp.zeros((256, 64), F32)], axis=1)
            tile = tile * s.cos[...] - swap_halves(tile) * s.sin[...]
            d_queries.append(tile.astype(BF16))
        d_query = jnp.concatenate(d_queries, axis=1)
        s.dq_pre[g] = d_query
        own_n1 = jnp.concatenate([s.n1[0, :, pl.ds(0, 128)], s.n1[1, :, pl.ds(0, 128)]], axis=1)
        grad = jnp.concatenate([grad, dot_nn(own_n1, d_query)], axis=1).astype(BF16)
        grad = dot_tn(s.spread[...], grad)
        if g == 0:
            tail = jnp.concatenate([jnp.zeros((DP_ROWS, 64), F32), out_tail], axis=1)
            grad = jnp.concatenate([grad[:, 0:128] + lines, grad[:, 128:256], grad[:, 256:384] + tail], axis=1)
        sums[g].begin(grad)
        if g == 0:
            out_sum.over_y()
        else:
            sums[g - 1].over_group()
            relay(g - 1)
            rs_second((None, 0, 2)[g])
    relay(2)
    sums[2].over_group()
    sums[0].over_y()

    net.arrived(out_slot, s.ahead_in, place.other_core())
    out = s.middle[...] + s.ahead[pl.ds(0, 256)] + s.ahead_in[...].astype(F32)
    for b in range(2):
        s.out_t[b] = jnp.transpose(out[128 * b : 128 * b + 128]).astype(BF16)
    out_copy = pltpu.make_async_copy(s.out_t, out_ref, s.local.at[2])
    out_copy.start()
    d_normed = jnp.zeros((256, D), F32)
    for g in range(3):
        d_normed += dot_nt(s.dq_pre[g], s.w_q[g])
    s.dn1[...] = d_normed
    rs_third(0)
    out_sum.over_group()
    sums[1].over_y()
    rs_third(2)
    sums[2].over_y()
    sums[0].over_pair()
    rs_second(1)

    s.dkv_sum[...] = dkv[:, :, 0].astype(F32)
    for g in range(3):
        for k in range(1, 8):

            @pl.when(rank + k <= 7)
            def _(k=k, g=g):
                net.arrived(dkv_slots[g][k], dkv_in.at[1, g, k], place.rank(k))
                s.dkv_sum[1, g] += dkv_in[1, g, k].astype(F32)
                if k % 2 == 0:
                    net.arrived(own_slots[g][k], dkv_in.at[0, g, k], place.rank(k))
                    s.dkv_sum[0, g] += dkv_in[0, g, k].astype(F32)

        net.arrived(cross_slots[g], s.cross_in.at[g], place.pair())
        s.dkv_sum[0, g] += s.cross_in[g].astype(F32)
    out_sum.over_pair()
    sums[1].over_pair()
    sums[2].over_pair()
    rs_third(1)
    d_pre = jnp.concatenate(
        [jnp.transpose(s.dkv_sum[b].reshape(384, 128)) for b in range(2)], axis=0
    )
    d_normed = s.dn1[...] + dot_nt(d_pre.astype(BF16), s.w_kv[...])
    inv1 = s.inv1[...]
    unit1 = s.x[...].astype(F32) * inv1
    scaled = d_normed * s.gain1[...]
    inner = jnp.sum(scaled * unit1, axis=1, keepdims=True) * (1.0 / D)
    d_in = s.d_middle[...] + inv1 * (scaled - unit1 * inner)
    for b in range(2):
        s.gx_t[b] = jnp.transpose(d_in[128 * b : 128 * b + 128]).astype(BF16)
    gx_copy = pltpu.make_async_copy(s.gx_t, gx_ref, s.local.at[3])
    gx_copy.start()

    out_sum.back()
    for g in range(3):
        total = sums[g].result()
        gk_ref[:, pl.ds(64 * g, 64)] = total[0:ROWS, 0:64]
        gv_ref[:, pl.ds(64 * g, 64)] = total[0:ROWS, 64:128]
        gq_ref[:, pl.ds(192 * g, 192)] = total[0:ROWS, 128:320]
        if g == 0:
            gnm_ref[...] = total[ROWS : ROWS + 1, 0:ROWS]
            go_ref[:, pl.ds(512, 64)] = total[0:ROWS, 320:384]
    rs_result()
    total = s.f[...]
    high = total.astype(BF16)
    low = (total - high.astype(F32)).astype(BF16)
    row, col = iota((12, PAD), 0), iota((12, PAD), 1)
    for t, ref in enumerate((gg_ref, gu_ref, gd_ref)):
        pick = one_hot(col == ((row >> 2) << 4) + 4 * t + (row & 3))
        ref[...] = dot_nn(pick, high) + dot_nn(pick, low)
    out_sum.result(go_ref)
    total = jnp.zeros((ROWS, 1), F32)
    for grad, weight in ((gq_ref, wq_ref), (gk_ref, wk_ref), (gv_ref, wv_ref)):
        total += jnp.sum(grad[...] * weight[...].astype(F32), axis=1, keepdims=True)
    total = jnp.transpose(jnp.broadcast_to(total, (ROWS, 128)))[0:1]
    gna_ref[...] = total / na_ref[...].astype(F32)
    out_copy.wait()
    gx_copy.wait()

    assert net.used <= COPIES, net.used
    net.finish()


def sum_buffers(width):
    shapes = [
        (2, 8, PAD, width),
        (8, PAD, width),
        (8, PAD, width),
        (7, PAD, width),
        (PAD, width),
        (3, PAD, width),
        (PAD, width),
        (PAD, width),
    ]
    return [pltpu.VMEM(shape, BF16) for shape in shapes]


def split_buffers():
    shapes = [
        (2, 4, 8, PAD, 128),
        (4, 8, PAD, 128),
        (4, 8, PAD, 128),
        (3, 8, PAD, 128),
        (8, PAD, 128),
        (7, PAD, 128),
        (PAD, 128),
        (PAD, 128),
        (4, PAD, 128),
    ]
    return [pltpu.VMEM(shape, BF16) for shape in shapes]


COPIES = 300

SCRATCH = dict(
    send=pltpu.SemaphoreType.DMA((COPIES,)),
    recv=pltpu.SemaphoreType.DMA((COPIES,)),
    local=pltpu.SemaphoreType.DMA((4,)),
    xs=pltpu.VMEM((8, 2, D, 128), BF16),
    dy_t=pltpu.VMEM((2, D, 128), BF16),
    out_t=pltpu.VMEM((2, D, 128), BF16),
    gx_t=pltpu.VMEM((2, D, 128), BF16),
    x=pltpu.VMEM((256, D), BF16),
    tile=pltpu.VMEM((3, 16, D), BF16),
    first=pltpu.VMEM((3, 4, 16, D), BF16),
    w=pltpu.VMEM((3, 4, 4, PAD, D), BF16),
    a_kv=pltpu.VMEM((BLOCKS, PAD, 384), BF16),
    a_q=pltpu.VMEM((BLOCKS, PAD, D), BF16),
    a_out=pltpu.VMEM((BLOCKS, PAD, D), BF16),
    w_kv=pltpu.VMEM((D, 384), BF16),
    w_q=pltpu.VMEM((3, D, 256), BF16),
    spread=pltpu.VMEM((D, DP_ROWS), BF16),
    seg=pltpu.VMEM((1024, 128), F32),
    cos=pltpu.VMEM((256, 128), F32),
    sin=pltpu.VMEM((256, 128), F32),
    cos_t=pltpu.VMEM((2, 32, 1024), F32),
    sin_t=pltpu.VMEM((2, 32, 1024), F32),
    bias=pltpu.VMEM((2, 128, 1024), F32),
    inv1=pltpu.VMEM((256, 1), F32),
    gain1=pltpu.VMEM((1, D), F32),
    gain2=pltpu.VMEM((1, D), F32),
    n1=pltpu.VMEM((2, D, 1024), BF16),
    q=pltpu.VMEM((3, 2, 128, 256), BF16),
    k=pltpu.VMEM((2, 3, 64, 1024), BF16),
    v=pltpu.VMEM((2, 3, 64, 1024), BF16),
    attn=pltpu.VMEM((2, 3, 384, 1024), BF16),
    inv_sum=pltpu.VMEM((2, 3, 384, 1), F32),
    mixed=pltpu.VMEM((2, 128, D), BF16),
    mixed_spread=pltpu.VMEM((256, DP_ROWS), BF16),
    middle=pltpu.VMEM((256, D), F32),
    inv2=pltpu.VMEM((256, 1), F32),
    n2=pltpu.VMEM((2, 256, D), BF16),
    dy=pltpu.VMEM((2, 256, D), BF16),
    dn2=pltpu.VMEM((512, D), F32),
    ahead=pltpu.VMEM((512, D), F32),
    dn2_out=pltpu.VMEM((256, D), BF16),
    dn2_in=pltpu.VMEM((256, D), BF16),
    ahead_out=pltpu.VMEM((256, D), BF16),
    ahead_in=pltpu.VMEM((256, D), BF16),
    d_middle=pltpu.VMEM((256, D), F32),
    d_mixed=pltpu.VMEM((2, 128, D), BF16),
    dq=pltpu.VMEM((256, 192), F32),
    dq_pre=pltpu.VMEM((3, 256, 256), BF16),
    dn1=pltpu.VMEM((256, D), F32),
    dkv=pltpu.VMEM((2, 3, 8, 128, 128), BF16),
    dkv_in=pltpu.VMEM((2, 3, 8, 128, 128), BF16),
    relay=pltpu.VMEM((3, 3, 128, 128), BF16),
    relay_sum=pltpu.VMEM((128, 128), F32),
    cross=pltpu.VMEM((3, 128, 128), BF16),
    cross_in=pltpu.VMEM((3, 128, 128), BF16),
    dkv_sum=pltpu.VMEM((2, 3, 128, 128), F32),
    g=pltpu.VMEM((3, 4, 4, PAD, D), BF16),
    ra=pltpu.VMEM((3, 3, 4, PAD, D), BF16),
    s2=pltpu.VMEM((3, 4, PAD, D), BF16),
    rb=pltpu.VMEM((3, 3, PAD, D), BF16),
    u=pltpu.VMEM((3, 4, 16, D), BF16),
    rc=pltpu.VMEM((3, 3, 16, D), BF16),
    f=pltpu.VMEM((PAD, D), F32),
    sum_out=split_buffers(),
    sums=[sum_buffers(384) for _ in range(3)],
)


def hand_over(*refs):
    count = len(refs) // 2
    for a, b in zip(refs[:count], refs[count:]):
        b[...] = a[...]


def local(
    inputs, segment_ids, norm_attn, w_query, w_key, w_value, w_out, norm_mlp, w_gate, w_up, w_down, cotangent,
):
    half = HEAD_WIDTH // 2
    freq = np.float32(ROPE_BASE) ** (-(np.float32(2.0) * np.arange(half, dtype=np.float32)) / HEAD_WIDTH)
    freq = freq.astype(np.float32)
    lane_freq = jnp.asarray(np.tile(freq, 4)[None, :])
    row_freq = jnp.asarray(np.tile(freq[:, None], (1, 128)))
    shapes = [
        ((2, D, 128), BF16),
        ((2, D, 128), BF16),
        ((1, ROWS), F32),
        ((ROWS, 576), F32),
        ((ROWS, 192), F32),
        ((ROWS, 192), F32),
        ((ROWS, D), F32),
        ((1, ROWS), F32),
        ((12, D), F32),
        ((12, D), F32),
        ((12, D), F32),
    ]
    shapes = [jax.ShapeDtypeStruct(shape, dtype) for shape, dtype in shapes]
    count = len(shapes)
    outs = pl.pallas_call(
        kernel,
        out_shape=shapes,
        in_specs=[pl.BlockSpec(memory_space=pl.ANY)] * 2 + [pl.BlockSpec(memory_space=pltpu.VMEM)] * 12,
        out_specs=[pl.BlockSpec(memory_space=pl.ANY)] * 2 + [pl.BlockSpec(memory_space=pltpu.VMEM)] * (count - 2),
        scratch_shapes=[SCRATCH],
        compiler_params=pltpu.CompilerParams(
            collective_id=0, has_side_effects=True, vmem_limit_bytes=60 * 2**20
        ),
        name="layer",
    )(
        jnp.transpose(inputs, (0, 2, 1)), jnp.transpose(cotangent, (0, 2, 1)), segment_ids, norm_attn[None, :],
        w_query, w_key, w_value, w_out, norm_mlp[None, :], w_gate.T, w_up.T, w_down, lane_freq, row_freq,
    )
    outs = pl.pallas_call(
        hand_over,
        out_shape=shapes,
        in_specs=[pl.BlockSpec(memory_space=pltpu.VMEM)] * count,
        out_specs=[pl.BlockSpec(memory_space=pltpu.VMEM)] * count,
        name="hand_over",
    )(*outs)
    outs = list(outs)
    for k in (0, 1):
        outs[k] = jnp.transpose(outs[k], (0, 2, 1))
    for k in (2, 7):
        outs[k] = outs[k].reshape(ROWS)
    for k in (8, 9):
        outs[k] = outs[k].T
    return tuple(outs)


def solution(mesh):
    rows, both = P("dp", None), ("dp", "seq")
    tokens = P("dp", "seq", None)
    weights = (P("dp"), rows, rows, rows, rows, P("dp"), P(None, both), P(None, both), P(both, None))
    return jax.shard_map(
        local,
        mesh=mesh,
        in_specs=(tokens, P("dp", None), *weights, tokens),
        out_specs=(tokens, tokens, *weights),
        check_vma=False,
    )
```

```python
import functools
import types

import jax
import jax.numpy as jnp
import numpy as np
from jax import lax
from jax.experimental import pallas as pl
from jax.experimental.pallas import tpu as pltpu
from jax.sharding import PartitionSpec as P

MESH = pl.DeviceIdType.MESH
F32 = jnp.float32
BF16 = jnp.bfloat16

D = 576
FF = 1536
QUERY_HEADS = 9
KV_HEADS = 3
HEAD_WIDTH = 64
ROPE_BASE = 100000.0
NORM_EPS = 1e-05
MASKED = -1e30

ROWS = 36
PAD = 48
BLOCKS = 16
DP_ROWS = BLOCKS * PAD
ORDERS = (("x", "y", "z"), ("y", "z", "x"), ("z", "x", "y"))
BACK = (("z", "y"), ("z", "x"), ("x", "y"))


def dot_nn(a, b):
    return lax.dot_general(a, b, (((1,), (0,)), ((), ())), preferred_element_type=F32)


def dot_nt(a, b):
    return lax.dot_general(a, b, (((1,), (1,)), ((), ())), preferred_element_type=F32)


def dot_tn(a, b):
    return lax.dot_general(a, b, (((0,), (0,)), ((), ())), preferred_element_type=F32)


def iota(shape, dim):
    return lax.broadcasted_iota(jnp.int32, shape, dim)


def one_hot(cond):
    return jnp.where(cond, 1.0, 0.0).astype(BF16)


class Place:
    def __init__(self):
        self.dp = lax.axis_index("dp")
        self.seq = lax.axis_index("seq")
        self.z = self.dp // 4
        self.x_hi = (self.dp // 2) % 2
        self.core = self.dp % 2
        self.y = self.seq // 2
        self.x_lo = self.seq % 2
        self.x = 2 * self.x_hi + self.x_lo

    def at(self, x, y, z, core):
        return (z * 4 + (x // 2) * 2 + core, y * 2 + x % 2)

    def coordinate(self, axis):
        return {"x": self.x, "y": self.y, "z": self.z}[axis]

    def ring(self, axis, step):
        here = {"x": self.x, "y": self.y, "z": self.z}
        here[axis] = (here[axis] + step + 4) % 4
        return self.at(here["x"], here["y"], here["z"], self.core)

    def other_core(self):
        return (self.dp + 1 - 2 * self.core, self.seq)

    def across(self):
        return self.at(3 - self.x, self.y, self.z, self.core)

    def group(self, dz, dx):
        z = (self.z + dz + 4) % 4
        x = 3 - self.x if dx else self.x
        return self.at(x, self.y, z, self.core), (z, x // 2)

    def pair(self):
        return self.at(self.x + 1 - 2 * self.x_lo, self.y, self.z, self.core)

    def rank(self, step):
        return (self.dp, (self.seq + step + 8) % 8)


class Net:
    def __init__(self, send, recv):
        self.send, self.recv, self.used = send, recv, 0
        self.unsent, self.maybe_unsent = [], []

    def new(self):
        self.used += 1
        return self.used - 1

    def copy(self, slot, src, dst, device):
        return pltpu.make_async_remote_copy(
            src_ref=src,
            dst_ref=dst,
            send_sem=self.send.at[slot],
            recv_sem=self.recv.at[slot],
            device_id=device,
            device_id_type=MESH,
        )

    def start(self, slot, src, dst, device):
        copy = self.copy(slot, src, dst, device)
        copy.start()
        self.unsent.append(copy)

    def arrived(self, slot, dst, device):
        self.copy(slot, dst, dst, device).wait_recv()

    def start_if(self, wanted, slot, src, dst, device):
        copy = self.copy(slot, src, dst, device)
        pl.when(wanted)(copy.start)
        self.maybe_unsent.append((wanted, copy))

    def arrived_if(self, wanted, slot, dst, device):
        pl.when(wanted)(functools.partial(self.arrived, slot, dst, device))

    def finish(self):
        for copy in self.unsent:
            copy.wait_send()
        for wanted, copy in self.maybe_unsent:
            pl.when(wanted)(copy.wait_send)


GROUP_STEPS = [(dz, dx) for dz in range(4) for dx in range(2) if (dz, dx) != (0, 0)]


class Summed:
    def __init__(self, net, place, refs):
        self.net, self.place = net, place
        (
            self.mine, self.from_core, self.chip, self.from_group, self.one, self.from_y, self.two, self.from_pair,
        ) = refs
        self.core_slot, self.pair_slot = net.new(), net.new()
        self.group_slots = [net.new() for _ in GROUP_STEPS]
        self.y_slots = [net.new() for _ in range(3)]

    def begin(self, value):
        place = self.place
        value = value.astype(BF16).reshape(4, 2, 2, PAD, value.shape[1])
        for c in range(2):
            self.mine[c] = value[:, :, c]
        self.net.start(
            self.core_slot, self.mine.at[1 - place.core], self.from_core, place.other_core()
        )

    def over_group(self):
        place, net = self.place, self.net
        net.arrived(self.core_slot, self.from_core, place.other_core())
        self.chip[...] = (
            self.mine[place.core].astype(F32) + self.from_core[...].astype(F32)
        ).astype(BF16)
        for k, (dz, dx) in enumerate(GROUP_STEPS):
            device, at = place.group(dz, dx)
            net.start(self.group_slots[k], self.chip.at[at], self.from_group.at[k], device)

    def over_y(self):
        place, net = self.place, self.net
        for k, (dz, dx) in enumerate(GROUP_STEPS):
            device, _ = place.group(-dz, dx)
            net.arrived(self.group_slots[k], self.from_group.at[k], device)
        total = self.chip[place.z, place.x_hi].astype(F32)
        for k in range(7):
            total += self.from_group[k].astype(F32)
        self.one[...] = total.astype(BF16)
        for d in (1, 2, 3):
            net.start(self.y_slots[d - 1], self.one, self.from_y.at[d - 1], place.ring("y", d))

    def over_pair(self):
        place, net = self.place, self.net
        for d in (1, 2, 3):
            net.arrived(self.y_slots[d - 1], self.from_y.at[d - 1], place.ring("y", -d))
        total = self.one[...].astype(F32)
        for d in range(3):
            total += self.from_y[d].astype(F32)
        self.two[...] = total.astype(BF16)
        net.start(self.pair_slot, self.two, self.from_pair, place.pair())

    def result(self):
        self.net.arrived(self.pair_slot, self.from_pair, self.place.pair())
        return self.two[...].astype(F32) + self.from_pair[...].astype(F32)


class SplitSummed:
    def __init__(self, net, place, refs):
        self.net, self.place = net, place
        (
            self.mine, self.from_core, self.chip, self.from_y, self.part, self.from_group, self.one, self.from_pair,
            self.whole,
        ) = refs
        self.core_slot, self.pair_slot = net.new(), net.new()
        self.y_slots = [net.new() for _ in range(3)]
        self.group_slots = [net.new() for _ in GROUP_STEPS]
        self.back_slots = [net.new() for _ in range(3)]

    def begin(self, value):
        place = self.place
        value = value.astype(BF16)
        for t in range(4):
            tile = value[:, 128 * t : 128 * t + 128].reshape(4, 2, 2, PAD, 128)
            for c in range(2):
                self.mine[c, t] = tile[:, :, c]
        self.net.start(
            self.core_slot, self.mine.at[1 - place.core], self.from_core, place.other_core()
        )

    def over_y(self):
        place, net = self.place, self.net
        net.arrived(self.core_slot, self.from_core, place.other_core())
        self.chip[...] = (
            self.mine[place.core].astype(F32) + self.from_core[...].astype(F32)
        ).astype(BF16)
        for d in (1, 2, 3):
            net.start(
                self.y_slots[d - 1],
                self.chip.at[(place.y + d) % 4],
                self.from_y.at[d - 1],
                place.ring("y", d),
            )

    def over_group(self):
        place, net = self.place, self.net
        for d in (1, 2, 3):
            net.arrived(self.y_slots[d - 1], self.from_y.at[d - 1], place.ring("y", -d))
        total = self.chip[place.y].astype(F32)
        for d in range(3):
            total += self.from_y[d].astype(F32)
        self.part[...] = total.astype(BF16)
        for k, (dz, dx) in enumerate(GROUP_STEPS):
            device, at = place.group(dz, dx)
            net.start(self.group_slots[k], self.part.at[at], self.from_group.at[k], device)

    def over_pair(self):
        place, net = self.place, self.net
        for k, (dz, dx) in enumerate(GROUP_STEPS):
            device, _ = place.group(-dz, dx)
            net.arrived(self.group_slots[k], self.from_group.at[k], device)
        total = self.part[place.z, place.x_hi].astype(F32)
        for k in range(7):
            total += self.from_group[k].astype(F32)
        self.one[...] = total.astype(BF16)
        net.start(self.pair_slot, self.one, self.from_pair, place.pair())

    def back(self):
        place, net = self.place, self.net
        net.arrived(self.pair_slot, self.from_pair, place.pair())
        total = self.one[...].astype(F32) + self.from_pair[...].astype(F32)
        self.whole[place.y] = total.astype(BF16)
        for d in (1, 2, 3):
            tile = self.whole.at[place.y]
            net.start(self.back_slots[d - 1], tile, tile, place.ring("y", d))

    def result(self, ref):
        place, net = self.place, self.net
        for d in (1, 2, 3):
            net.arrived(
                self.back_slots[d - 1], self.whole.at[(place.y + 4 - d) % 4], place.ring("y", -d)
            )
        for t in range(4):
            ref[:, pl.ds(128 * t, 128)] = self.whole[t, pl.ds(0, ROWS)].astype(F32)


class Gathered:
    def __init__(self, net, place, whole):
        self.net, self.place, self.whole = net, place, whole
        self.group_slots = [net.new() for _ in GROUP_STEPS]
        self.core_slots = [net.new() for _ in range(8)]

    def begin(self):
        place, net = self.place, self.net
        block = self.whole.at[place.z, place.x_hi, place.core]
        for k, (dz, dx) in enumerate(GROUP_STEPS):
            net.start(self.group_slots[k], block, block, place.group(dz, dx)[0])
        net.start(self.core_slots[7], block, block, place.other_core())

    def pass_on(self):
        place, net = self.place, self.net
        for k, (dz, dx) in enumerate(GROUP_STEPS):
            device, at = place.group(-dz, dx)
            block = self.whole.at[(*at, place.core)]
            net.arrived(self.group_slots[k], block, device)
            net.start(self.core_slots[k], block, block, place.other_core())

    def finish(self):
        place, net = self.place, self.net
        for k, (dz, dx) in enumerate(GROUP_STEPS):
            _, at = place.group(-dz, dx)
            net.arrived(self.core_slots[k], self.whole.at[(*at, 1 - place.core)], place.other_core())
        block = self.whole.at[place.z, place.x_hi, 1 - place.core]
        net.arrived(self.core_slots[7], block, place.other_core())


def swap_halves(tile):
    first = (iota(tile.shape, 1) & 32) == 0
    return jnp.where(first, pltpu.roll(tile, 96, 1), pltpu.roll(tile, 32, 1))


def kernel(
    x_ref, dy_ref, seg_ref, na_ref, wq_ref, wk_ref, wv_ref, wo_ref, nm_ref, wg_ref, wu_ref, wd_ref, lane_freq_ref,
    row_freq_ref,
    out_ref, gx_ref, gna_ref, gq_ref, gk_ref, gv_ref, go_ref, gnm_ref, gg_ref, gu_ref, gd_ref,
    s,
):
    s = types.SimpleNamespace(**s)
    place = Place()
    net = Net(s.send, s.recv)
    rank = place.seq
    apart = place.x_lo == 0
    xs = s.xs

    barrier = pltpu.get_barrier_semaphore()
    peers = [place.ring(axis, step) for axis in "xyz" for step in (1, 2, 3)]
    peers += [place.other_core()]
    peers += [place.group(dz, 1)[0] for dz in (1, 2, 3)]
    for peer in peers:
        pl.semaphore_signal(barrier, inc=1, device_id=peer, device_id_type=MESH)
    x_copy = pltpu.make_async_copy(x_ref, xs.at[0], s.local.at[0])
    dy_copy = pltpu.make_async_copy(dy_ref, s.dy_t, s.local.at[1])
    x_copy.start()
    dy_copy.start()

    a_kv, a_q, a_out = s.a_kv, s.a_q, s.a_out
    down = one_hot(iota((PAD, ROWS), 0) == iota((PAD, ROWS), 1))
    keys, values = dot_nn(down, wk_ref[...]), dot_nn(down, wv_ref[...])
    widen = one_hot(iota((ROWS, 128), 0) == iota((ROWS, 128), 1))
    row = iota((PAD, 128), 0)
    for g in range(3):
        tile = jnp.concatenate([keys[:, 64 * g : 64 * g + 64], values[:, 64 * g : 64 * g + 64]], axis=1)
        if g == 0:
            for k, ref in enumerate((na_ref, nm_ref)):
                line = dot_nn(jnp.broadcast_to(ref[...], (16, ROWS)), widen)[0:1]
                tile = tile + jnp.where(row == ROWS + k, line, 0.0)
        a_kv[place.z, place.x_hi, place.core, :, pl.ds(128 * g, 128)] = tile.astype(BF16)
    a_q[place.z, place.x_hi, place.core] = dot_nn(down, wq_ref[...]).astype(BF16)
    a_out[place.z, place.x_hi, place.core] = dot_nn(down, wo_ref[...]).astype(BF16)

    row, col = iota((16, 12), 0), iota((16, 12), 1)
    for p in range(3):
        tile = jnp.zeros((16, D), F32)
        for t, ref in enumerate((wg_ref, wu_ref, wd_ref)):
            pick = one_hot(((row >> 2) == t) & (col == 4 * p + (row & 3)))
            tile += dot_nn(pick, ref[...])
        s.tile[p] = tile.astype(BF16)

    kv_weights, q_weights, out_weights = (Gathered(net, place, a) for a in (a_kv, a_q, a_out))
    ff_slots = [[[net.new() for _ in range(3)] for _ in range(4)] for _ in range(3)]
    dy_slot, n2_slot, out_slot, dn2_slot = (net.new() for _ in range(4))
    swap_slot = net.new()
    x_slots = [net.new() for _ in range(8)]
    relayed_slots = [net.new() for _ in range(8)]
    column_slots = [net.new() for _ in range(8)]
    across_slots = [net.new() for _ in range(8)]

    x_copy.wait()
    pl.semaphore_wait(barrier, len(peers))

    for p, (one, _, _) in enumerate(ORDERS):
        mine = place.coordinate(one)
        s.first[p, mine] = s.tile[p]
        for d in (1, 2, 3):
            net.start(
                ff_slots[p][0][d - 1], s.tile.at[p], s.first.at[p, mine], place.ring(one, d)
            )
    kv_weights.begin()
    net.start(swap_slot, xs.at[0, 0], s.swapped, place.pair())
    for k in (2, 6, 4):
        net.start_if(rank + k <= 7, column_slots[k], xs.at[0, 1], xs.at[k, 1], place.rank(k))
    for k in (2, 6, 4):
        net.start_if(rank + k <= 7, x_slots[k], xs.at[0, 0], xs.at[k, 0], place.rank(k))
    net.start_if(apart, across_slots[1], xs.at[0, 1], xs.at[1, 1], place.pair())
    q_weights.begin()
    dy_copy.wait()
    for b in range(2):
        s.x[pl.ds(128 * b, 128)] = jnp.transpose(xs[0, b].astype(F32)).astype(BF16)
        s.dy[0, pl.ds(128 * b, 128)] = jnp.transpose(s.dy_t[b].astype(F32)).astype(BF16)
    net.start(dy_slot, s.dy.at[0], s.dy.at[1], place.other_core())

    row, col = iota((PAD, 64), 0), iota((PAD, 64), 1)
    pack = one_hot(col == (((row >> 2) & 3) << 4) + ((row >> 4) << 2) + (row & 3))
    row, col = iota((64, PAD), 0), iota((64, PAD), 1)
    unpack = one_hot(row == (((col >> 2) & 3) << 4) + ((col >> 4) << 2) + (col & 3))

    def ff_second():
        for p, (one, two, three) in enumerate(ORDERS):
            mine = place.coordinate(one)
            for d in (1, 2, 3):
                net.arrived(
                    ff_slots[p][0][d - 1], s.first.at[p, (mine + 4 - d) % 4], place.ring(one, -d)
                )
            block = s.w.at[p, place.coordinate(three), place.coordinate(two)]
            block[...] = dot_nn(pack, s.first[p].reshape(64, D)).astype(BF16)
            for d in (1, 2, 3):
                net.start(ff_slots[p][1][d - 1], block, block, place.ring(two, d))

    def ff_third(p):
        _, two, three = ORDERS[p]
        mine, last = place.coordinate(two), place.coordinate(three)
        for d in (1, 2, 3):
            net.arrived(
                ff_slots[p][1][d - 1], s.w.at[p, last, (mine + 4 - d) % 4], place.ring(two, -d)
            )
        block = s.w.at[p, last]
        net.start(ff_slots[p][2][0], block, block, place.ring(three, 1))
        net.start(ff_slots[p][2][1], block, block, place.ring(three, -1))

    def ff_past(p):
        three = ORDERS[p][2]
        last = place.coordinate(three)
        for way, step in enumerate((1, -1)):
            come = (last + 4 - step) % 4
            net.arrived(ff_slots[p][2][way], s.w.at[p, come], place.ring(three, -step))
            half = s.w.at[p, come, pl.ds(2 * way, 2)]
            net.start(ff_slots[p][3][way], half, half, place.ring(three, step))

    def ff_have(p):
        three = ORDERS[p][2]
        last = (place.coordinate(three) + 2) % 4
        for way, step in enumerate((1, -1)):
            half = s.w.at[p, last, pl.ds(2 * way, 2)]
            net.arrived(ff_slots[p][3][way], half, place.ring(three, -step))

    for k in range(1, 8):

        @pl.when(k > rank)
        def _(k=k):
            xs[k] = jnp.zeros((2, D, 128), BF16)

    ff_second()
    net.arrived(swap_slot, s.swapped, place.pair())
    for k in (2, 6, 4):
        there = xs.at[k - 1 + 2 * place.x_lo, 0]
        net.start_if(rank + k <= 7, relayed_slots[k], s.swapped, there, place.rank(k))

    @pl.when(jnp.logical_not(apart))
    def _():
        xs[1, 0] = s.swapped[...]

    row = iota((D, DP_ROWS), 0).astype(F32)
    col = iota((D, DP_ROWS), 1).astype(F32)
    s.spread[...] = one_hot(col - row == 12.0 * jnp.floor((row + 0.5) * (1.0 / ROWS)))
    def tables(b):
        lane = iota((128, 128), 1)
        own = seg_ref[pl.ds(b, 1), pl.ds(pl.multiple_of(rank * 128, 128), 128)].astype(F32)
        own = jnp.transpose(jnp.broadcast_to(own, (128, 128)))
        earlier = jnp.zeros((128, 128), F32)
        for c in range(8):
            part = seg_ref[pl.ds(b, 1), pl.ds(128 * c, 128)].astype(F32)
            earlier += jnp.where(part < own, 1.0, 0.0)
            s.seg[pl.ds(128 * c, 128)] = jnp.transpose(jnp.broadcast_to(part, (128, 128)))
        begin = jnp.sum(earlier, axis=1, keepdims=True)
        here = (iota((128, 1), 0) + rank * 128).astype(F32)
        angle = (here - begin) * lane_freq_ref[...]
        s.cos[pl.ds(128 * b, 128)] = jnp.cos(angle)
        sine = jnp.sin(angle)
        s.sin[pl.ds(128 * b, 128)] = jnp.where((lane & 32) == 0, -sine, sine)
        for k in range(8):
            key = (lane + 128 * (rank - k)).astype(F32)
            s.bias[b, :, pl.ds(128 * k, 128)] = jnp.where(
                (key >= begin) & (key <= here), 0.0, MASKED
            )
            first = pl.multiple_of(jnp.maximum(rank - k, 0) * 128, 128)
            part = seg_ref[pl.ds(b, 1), pl.ds(first, 128)].astype(F32)
            begins = jnp.sum(jnp.where(s.seg[...] < part, 1.0, 0.0), axis=0, keepdims=True)
            angle = ((iota((1, 128), 1) + first).astype(F32) - begins) * row_freq_ref[...]
            s.cos_t[b, :, pl.ds(128 * k, 128)] = jnp.cos(angle)
            s.sin_t[b, :, pl.ds(128 * k, 128)] = jnp.sin(angle)

    x32 = s.x[...].astype(F32)
    s.inv1[...] = lax.rsqrt(jnp.sum(x32 * x32, axis=1, keepdims=True) * (1.0 / D) + NORM_EPS)

    kv_weights.pass_on()
    for k in (2, 6, 4):
        net.arrived_if(k <= rank, column_slots[k], xs.at[k, 1], place.rank(-k))
        here = k <= rank
        net.start_if(here & apart, across_slots[k + 1], xs.at[k, 1], xs.at[k + 1, 1], place.pair())
        net.start_if(
            here & jnp.logical_not(apart), across_slots[k - 1], xs.at[k, 1], xs.at[k - 1, 1], place.pair()
        )
    for p in range(3):
        ff_third(p)
    out_weights.begin()
    tables(0)
    q_weights.pass_on()
    tables(1)
    kv_weights.finish()

    spread = s.spread[...]
    row, col = iota((BLOCKS, DP_ROWS), 0), iota((BLOCKS, DP_ROWS), 1)
    a_kv_tile = a_kv[:, :, :, :, pl.ds(0, 128)].reshape(DP_ROWS, 128)
    line1, line2 = (
        dot_nn(one_hot(col == row * PAD + ROWS + k), a_kv_tile).astype(BF16) for k in range(2)
    )
    row, col = iota((D, 128), 0).astype(F32), iota((D, 128), 1).astype(F32)
    within = one_hot(row - ROWS * jnp.floor((row + 0.5) * (1.0 / ROWS)) == col)
    row, col = iota((BLOCKS, D), 0), iota((BLOCKS, D), 1)
    block = (col >= row * ROWS) & (col < row * ROWS + ROWS)
    gain1, gain2 = (
        jnp.sum(jnp.where(block, dot_nt(line, within), 0.0), axis=0, keepdims=True) for line in (line1, line2)
    )
    s.gain1[...] = gain1
    s.gain2[...] = gain2
    row, col = iota((D, BLOCKS), 0), iota((D, BLOCKS), 1)
    block_t = (row >= col * ROWS) & (row < col * ROWS + ROWS)
    gain1_t = jnp.sum(jnp.where(block_t, dot_nt(within, line1), 0.0), axis=1, keepdims=True)
    s.w_kv[...] = dot_nn(spread, a_kv[...].reshape(DP_ROWS, 384)).astype(BF16)
    q_weights.finish()
    w_q = dot_nn(spread, a_q[...].reshape(DP_ROWS, D))
    for g in range(3):
        part = [w_q[:, 192 * g : 192 * g + 192], jnp.zeros((D, 64), F32)]
        s.w_q[g] = jnp.concatenate(part, axis=1).astype(BF16)

    n1 = s.x[...].astype(F32) * s.inv1[...] * gain1
    n1 = n1.astype(BF16)
    for g in range(3):
        pre = dot_nn(n1, s.w_q[g])
        for t in range(2):
            tile = pre[:, 128 * t : 128 * t + 128]
            tile = tile * s.cos[...] + swap_halves(tile) * s.sin[...]
            tile = (tile * HEAD_WIDTH**-0.5).astype(BF16).reshape(2, 128, 128)
            s.q[g, :, :, pl.ds(128 * t, 128)] = tile

    for p in range(3):
        ff_past(p)

    def heads(value, first):
        return jnp.concatenate(
            [value[:, 64 * h : 64 * h + 64] for h in range(first, first + 3)], axis=0
        )

    def turned(value, b, back):
        cos, sin = s.cos_t[b], s.sin_t[b]
        one, two = value[0:32], value[32:64]
        if back:
            return one * cos + two * sin, two * cos - one * sin
        return one * cos - two * sin, two * cos + one * sin

    for b in range(2):
        if b == 0:
            for k in (2, 6, 4):
                net.arrived_if(k <= rank, x_slots[k], xs.at[k, 0], place.rank(-k))
                there = xs.at[k - 1 + 2 * place.x_lo, 0]
                net.arrived_if(k <= rank, relayed_slots[k], there, place.rank(-k))
        else:
            for k in (1, 3, 5, 7):
                net.arrived_if(k <= rank, across_slots[k], xs.at[k, 1], place.pair())
        for k in range(8):
            part = xs[k, b].astype(F32)
            inv = lax.rsqrt(jnp.sum(part * part, axis=0, keepdims=True) * (1.0 / D) + NORM_EPS)
            s.n1[b, :, pl.ds(128 * k, 128)] = (part * inv * gain1_t).astype(BF16)
        both = dot_tn(s.w_kv[...], s.n1[b])
        for g in range(3):
            one, two = turned(both[128 * g : 128 * g + 64], b, False)
            s.k[b, g, pl.ds(0, 32)] = one.astype(BF16)
            s.k[b, g, pl.ds(32, 32)] = two.astype(BF16)
            s.v[b, g] = both[128 * g + 64 : 128 * g + 128].astype(BF16)

    out_weights.pass_on()

    @pl.loop(0, 2)
    def _(b):
        bias = s.bias[b]
        for g in range(3):
            query = heads(s.q[g, b], 0)
            score = dot_nn(query, s.k[b, g])
            score = (score.reshape(3, 128, 1024) + bias[None]).reshape(384, 1024)
            top = jnp.max(score, axis=1, keepdims=True)
            score = jnp.exp(score - top)
            inv = 1.0 / jnp.sum(score, axis=1, keepdims=True)
            weight = score.astype(BF16)
            s.attn[b, g] = weight
            s.inv_sum[b, g] = inv
            mixed = (dot_nt(weight, s.v[b, g]) * inv).astype(BF16)
            for h in range(3):
                s.mixed[b, :, pl.ds(64 * (3 * g + h), 64)] = mixed[128 * h : 128 * h + 128]

    out_weights.finish()
    w_out = a_out[...].reshape(DP_ROWS, D)
    s.mixed_spread[...] = dot_nn(s.mixed[...].reshape(256, D), s.spread[...]).astype(BF16)
    middle = s.x[...].astype(F32) + dot_nn(s.mixed_spread[...], w_out)
    s.middle[...] = middle
    inv2 = lax.rsqrt(jnp.sum(middle * middle, axis=1, keepdims=True) * (1.0 / D) + NORM_EPS)
    s.inv2[...] = inv2
    s.n2[0] = (middle * inv2 * s.gain2[...]).astype(BF16)
    net.start(n2_slot, s.n2.at[0], s.n2.at[1], place.other_core())
    net.arrived(dy_slot, s.dy.at[1], place.other_core())
    net.arrived(n2_slot, s.n2.at[1], place.other_core())

    rs_slots = [[[net.new() for _ in range(6)] for _ in range(3)] for _ in range(3)]

    def chunk(p, step, half):
        there = (place.coordinate(BACK[p][0]) + step + 4) % 4
        if BACK[p][0] == ORDERS[p][2]:
            return s.g.at[p, there, pl.ds(2 * half, 2)]
        return s.g.at[p, pl.ds(2 * half, 2), there]

    def rs_first(p):
        axis, slots = BACK[p][0], rs_slots[p][0]
        for way, step in enumerate((1, -1)):
            device = place.ring(axis, step)
            net.start(slots[way], chunk(p, 2, way), s.ra.at[p, way], device)
            net.start(slots[2 + way], chunk(p, step, 1 - way), s.ra.at[p, 2 + way], device)

    def rs_past(p):
        axis, slots = BACK[p][0], rs_slots[p][0]
        for way, step in enumerate((1, -1)):
            net.arrived(slots[way], s.ra.at[p, way], place.ring(axis, -step))
            total = chunk(p, step, way)[...].astype(F32) + s.ra[p, way].astype(F32)
            s.rp[p, way] = total.astype(BF16)
            net.start(slots[4 + way], s.rp.at[p, way], s.ra.at[p, 4 + way], place.ring(axis, step))

    normed, upper = s.n2[...].reshape(512, D), s.dy[...].reshape(512, D)
    for p in (0, 2, 1):
        ff_have(p)
        w_gate, w_up, w_down = (
            s.w[p, :, :, pl.ds(16 * t, 16), :].reshape(256, D) for t in range(3)
        )
        gate = dot_nt(normed, w_gate)
        up = dot_nt(normed, w_up)
        d_act = dot_nt(upper, w_down)
        sigmoid = 1.0 / (1.0 + jnp.exp(-gate))
        silu = gate * sigmoid
        act = (silu * up).astype(BF16)
        d_gate = (d_act * up * sigmoid * (1.0 + gate * (1.0 - sigmoid))).astype(BF16)
        d_up = (d_act * silu).astype(BF16)
        back = dot_nn(d_gate, w_gate) + dot_nn(d_up, w_up)
        ahead = dot_nn(act, w_down)
        if p == 0:
            s.dn2[...] = back
            s.ahead[...] = ahead
        else:
            s.dn2[...] += back
            s.ahead[...] += ahead
        for t, (left, right) in enumerate(((d_gate, normed), (d_up, normed), (act, upper))):
            s.g[p, :, :, pl.ds(16 * t, 16), :] = (
                dot_tn(left, right).astype(BF16).reshape(4, 4, 16, D)
            )
        rs_first(p)
    s.dn2_out[...] = s.dn2[pl.ds(256, 256)].astype(BF16)
    net.start(dn2_slot, s.dn2_out, s.dn2_in, place.other_core())
    s.ahead_out[...] = s.ahead[pl.ds(256, 256)].astype(BF16)
    net.start(out_slot, s.ahead_out, s.ahead_in, place.other_core())

    def rs_second(p):
        first, second = BACK[p]
        for way, step in enumerate((1, -1)):
            net.arrived(rs_slots[p][0][2 + way], s.ra.at[p, 2 + way], place.ring(first, -step))
            net.arrived(rs_slots[p][0][4 + way], s.ra.at[p, 4 + way], place.ring(first, -step))
        for half in range(2):
            total = chunk(p, 0, half)[...].astype(F32)
            total += s.ra[p, 3 - half].astype(F32) + s.ra[p, 4 + half].astype(F32)
            s.s2[p, pl.ds(2 * half, 2)] = total.astype(BF16)
        mine = place.coordinate(second)
        for d in (1, 2, 3):
            net.start(
                rs_slots[p][1][d - 1],
                s.s2.at[p, (mine + d) % 4],
                s.rb.at[p, d - 1],
                place.ring(second, d),
            )

    def rs_third(p):
        one, second = ORDERS[p][0], BACK[p][1]
        for d in (1, 2, 3):
            net.arrived(rs_slots[p][1][d - 1], s.rb.at[p, d - 1], place.ring(second, -d))
        total = s.s2[p, place.coordinate(second)].astype(F32)
        for d in range(3):
            total += s.rb[p, d].astype(F32)
        s.u[p] = dot_nn(unpack, total.astype(BF16)).astype(BF16).reshape(4, 16, D)
        mine = place.coordinate(one)
        for d in (1, 2, 3):
            net.start(
                rs_slots[p][2][d - 1],
                s.u.at[p, (mine + d) % 4],
                s.rc.at[p, d - 1],
                place.ring(one, d),
            )

    def rs_result():
        for p, (one, _, _) in enumerate(ORDERS):
            for d in (1, 2, 3):
                net.arrived(rs_slots[p][2][d - 1], s.rc.at[p, d - 1], place.ring(one, -d))
            total = s.u[p, place.coordinate(one)].astype(F32)
            for d in range(3):
                total += s.rc[p, d].astype(F32)
            s.f[pl.ds(16 * p, 16)] = total

    net.arrived(dn2_slot, s.dn2_in, place.other_core())
    d_normed = s.dn2[pl.ds(0, 256)] + s.dn2_in[...].astype(F32)
    middle, inv2 = s.middle[...], s.inv2[...]
    unit2 = middle * inv2
    scaled = d_normed * s.gain2[...]
    inner = jnp.sum(scaled * unit2, axis=1, keepdims=True) * (1.0 / D)
    d_middle = s.dy[0].astype(F32) + inv2 * (scaled - unit2 * inner)
    s.d_middle[...] = d_middle
    g_gain2 = jnp.sum(d_normed * unit2, axis=0, keepdims=True)
    d_branch = d_middle.astype(BF16)
    w_out = a_out[...].reshape(DP_ROWS, D)
    d_mixed = dot_nt(d_branch, w_out).astype(BF16)
    s.d_mixed[...] = dot_nt(d_mixed, s.spread[...]).astype(BF16).reshape(2, 128, D)
    out_sum = SplitSummed(net, place, s.sum_out)
    grad = dot_tn(s.mixed_spread[...], d_branch)
    out_sum.begin(grad[:, 0:512])
    out_tail = grad[:, 512:576]
    lines = dot_nn(jnp.where(block, g_gain2, 0.0).astype(BF16), within).astype(BF16)
    row, col = iota((DP_ROWS, BLOCKS), 0), iota((DP_ROWS, BLOCKS), 1)
    lines = dot_nn(one_hot(row == col * PAD + ROWS), lines)

    dkv, dkv_in = s.dkv, s.dkv_in
    own_slots = [[net.new() for _ in range(8)] for _ in range(3)]
    relay_slots = [[net.new() for _ in range(8)] for _ in range(3)]
    cross_slots = [net.new() for _ in range(3)]
    sums = [Summed(net, place, s.sums[g]) for g in range(3)]

    def relay(g):
        total = s.relay_sum
        total[...] = jnp.where(place.x_lo == 1, dkv[g, 1].astype(F32), 0.0)
        for k in (2, 4, 6):

            @pl.when(rank + k <= 7)
            def _(k=k):
                net.arrived(relay_slots[g][k], s.relay.at[g, k // 2 - 1], place.rank(k))
                total[...] += s.relay[g, k // 2 - 1].astype(F32)

        s.cross[g] = total[...].astype(BF16)
        net.start(cross_slots[g], s.cross.at[g], s.cross_in.at[g], place.pair())

    for g in range(3):
        s.grad[...] = jnp.zeros((D, 128), F32)

        @pl.loop(0, 2)
        def _(b, g=g):
            inv = s.inv_sum[b, g]
            query = heads(s.q[g, b], 0)
            d_out = (heads(s.d_mixed[b], 3 * g).astype(F32) * inv).astype(BF16)
            inner = jnp.sum(
                d_out.astype(F32) * heads(s.mixed[b], 3 * g).astype(F32), axis=1, keepdims=True
            )
            weight = s.attn[b, g]
            d_score = (weight.astype(F32) * (dot_nn(d_out, s.v[b, g]) - inner)).astype(BF16)
            d_query = dot_nt(d_score, s.k[b, g]) * HEAD_WIDTH**-0.5
            for h in range(3):
                s.dq[pl.ds(pl.multiple_of(128 * b, 128), 128), pl.ds(64 * h, 64)] = d_query[128 * h : 128 * h + 128]
            one, two = turned(dot_tn(query, d_score), b, True)
            both = jnp.concatenate([one, two, dot_tn(d_out, weight)], axis=0).astype(BF16)
            for k in range(8):
                dkv[g, k, b] = both[:, 128 * k : 128 * k + 128]
            s.grad[...] += dot_nt(s.n1[b], both)

        for k in (2, 6, 4):
            here = k <= rank
            at = k // 2 - 1
            net.start_if(here, own_slots[g][k], dkv.at[g, k], dkv_in.at[g, at], place.rank(-k))
            other = dkv.at[g, k - 1 + 2 * place.x_lo]
            net.start_if(here, relay_slots[g][k], other, s.relay.at[g, at], place.rank(-k))
        d_queries = []
        for t in range(2):
            if t == 0:
                tile = s.dq[:, pl.ds(0, 128)]
            else:
                tile = jnp.concatenate([s.dq[:, pl.ds(128, 64)], jnp.zeros((256, 64), F32)], axis=1)
            tile = tile * s.cos[...] - swap_halves(tile) * s.sin[...]
            d_queries.append(tile.astype(BF16))
        d_query = jnp.concatenate(d_queries, axis=1)
        s.dq_pre[g] = d_query
        own_n1 = jnp.concatenate([s.n1[0, :, pl.ds(0, 128)], s.n1[1, :, pl.ds(0, 128)]], axis=1)
        grad = jnp.concatenate([s.grad[...], dot_nn(own_n1, d_query)], axis=1).astype(BF16)
        grad = dot_tn(s.spread[...], grad)
        if g == 0:
            tail = jnp.concatenate([jnp.zeros((DP_ROWS, 64), F32), out_tail], axis=1)
            grad = jnp.concatenate([grad[:, 0:128] + lines, grad[:, 128:256], grad[:, 256:384] + tail], axis=1)
        sums[g].begin(grad)
        if g == 0:
            out_sum.over_y()
            rs_past(0)
            rs_past(2)
        elif g == 1:
            sums[0].over_group()
            rs_past(1)
        else:
            sums[1].over_group()
            out_sum.over_group()
    sums[2].over_group()
    rs_second(0)
    rs_second(2)
    sums[0].over_y()

    net.arrived(out_slot, s.ahead_in, place.other_core())
    out = s.middle[...] + s.ahead[pl.ds(0, 256)] + s.ahead_in[...].astype(F32)
    for b in range(2):
        s.out_t[b] = jnp.transpose(out[128 * b : 128 * b + 128]).astype(BF16)
    out_copy = pltpu.make_async_copy(s.out_t, out_ref, s.local.at[2])
    out_copy.start()
    d_normed = jnp.zeros((256, D), F32)
    for g in range(3):
        d_normed += dot_nt(s.dq_pre[g], s.w_q[g])
    s.dn1[...] = d_normed
    for g in range(3):
        relay(g)
    rs_second(1)
    sums[1].over_y()
    out_sum.over_pair()
    sums[0].over_pair()
    rs_third(0)
    rs_third(2)
    sums[2].over_y()

    s.dkv_sum[...] = dkv[:, 0].astype(F32)
    for g in range(3):
        for k in (2, 4, 6):

            @pl.when(rank + k <= 7)
            def _(k=k, g=g):
                net.arrived(own_slots[g][k], dkv_in.at[g, k // 2 - 1], place.rank(k))
                s.dkv_sum[g] += dkv_in[g, k // 2 - 1].astype(F32)

        net.arrived(cross_slots[g], s.cross_in.at[g], place.pair())
        s.dkv_sum[g] += s.cross_in[g].astype(F32)
    sums[1].over_pair()
    out_sum.back()
    rs_third(1)
    sums[2].over_pair()
    d_pre = jnp.concatenate(
        [jnp.transpose(s.dkv_sum[:, b].reshape(384, 128)) for b in range(2)], axis=0
    )
    d_normed = s.dn1[...] + dot_nt(d_pre.astype(BF16), s.w_kv[...])
    inv1 = s.inv1[...]
    unit1 = s.x[...].astype(F32) * inv1
    scaled = d_normed * s.gain1[...]
    inner = jnp.sum(scaled * unit1, axis=1, keepdims=True) * (1.0 / D)
    d_in = s.d_middle[...] + inv1 * (scaled - unit1 * inner)
    for b in range(2):
        s.gx_t[b] = jnp.transpose(d_in[128 * b : 128 * b + 128]).astype(BF16)
    gx_copy = pltpu.make_async_copy(s.gx_t, gx_ref, s.local.at[3])
    gx_copy.start()

    for g in range(3):
        total = sums[g].result()
        gk_ref[:, pl.ds(64 * g, 64)] = total[0:ROWS, 0:64]
        gv_ref[:, pl.ds(64 * g, 64)] = total[0:ROWS, 64:128]
        gq_ref[:, pl.ds(192 * g, 192)] = total[0:ROWS, 128:320]
        if g == 0:
            gnm_ref[...] = total[ROWS : ROWS + 1, 0:ROWS]
            go_ref[:, pl.ds(512, 64)] = total[0:ROWS, 320:384]
    rs_result()
    total = s.f[...]
    high = total.astype(BF16)
    low = (total - high.astype(F32)).astype(BF16)
    row, col = iota((12, PAD), 0), iota((12, PAD), 1)
    for t, ref in enumerate((gg_ref, gu_ref, gd_ref)):
        pick = one_hot(col == ((row >> 2) << 4) + 4 * t + (row & 3))
        ref[...] = dot_nn(pick, high) + dot_nn(pick, low)
    out_sum.result(go_ref)
    total = jnp.zeros((ROWS, 1), F32)
    for grad, weight in ((gq_ref, wq_ref), (gk_ref, wk_ref), (gv_ref, wv_ref)):
        total += jnp.sum(grad[...] * weight[...].astype(F32), axis=1, keepdims=True)
    total = jnp.transpose(jnp.broadcast_to(total, (ROWS, 128)))[0:1]
    gna_ref[...] = total / na_ref[...].astype(F32)
    out_copy.wait()
    gx_copy.wait()

    assert net.used <= COPIES, net.used
    net.finish()


def sum_buffers(width):
    shapes = [
        (2, 4, 2, PAD, width),
        (4, 2, PAD, width),
        (4, 2, PAD, width),
        (7, PAD, width),
        (PAD, width),
        (3, PAD, width),
        (PAD, width),
        (PAD, width),
    ]
    return [pltpu.VMEM(shape, BF16) for shape in shapes]


def split_buffers():
    shapes = [
        (2, 4, 4, 2, PAD, 128),
        (4, 4, 2, PAD, 128),
        (4, 4, 2, PAD, 128),
        (3, 4, 2, PAD, 128),
        (4, 2, PAD, 128),
        (7, PAD, 128),
        (PAD, 128),
        (PAD, 128),
        (4, PAD, 128),
    ]
    return [pltpu.VMEM(shape, BF16) for shape in shapes]


COPIES = 300

SCRATCH = dict(
    send=pltpu.SemaphoreType.DMA((COPIES,)),
    recv=pltpu.SemaphoreType.DMA((COPIES,)),
    local=pltpu.SemaphoreType.DMA((4,)),
    xs=pltpu.VMEM((8, 2, D, 128), BF16),
    swapped=pltpu.VMEM((D, 128), BF16),
    dy_t=pltpu.VMEM((2, D, 128), BF16),
    out_t=pltpu.VMEM((2, D, 128), BF16),
    gx_t=pltpu.VMEM((2, D, 128), BF16),
    x=pltpu.VMEM((256, D), BF16),
    tile=pltpu.VMEM((3, 16, D), BF16),
    first=pltpu.VMEM((3, 4, 16, D), BF16),
    w=pltpu.VMEM((3, 4, 4, PAD, D), BF16),
    a_kv=pltpu.VMEM((4, 2, 2, PAD, 384), BF16),
    a_q=pltpu.VMEM((4, 2, 2, PAD, D), BF16),
    a_out=pltpu.VMEM((4, 2, 2, PAD, D), BF16),
    w_kv=pltpu.VMEM((D, 384), BF16),
    w_q=pltpu.VMEM((3, D, 256), BF16),
    spread=pltpu.VMEM((D, DP_ROWS), BF16),
    seg=pltpu.VMEM((1024, 128), F32),
    cos=pltpu.VMEM((256, 128), F32),
    sin=pltpu.VMEM((256, 128), F32),
    cos_t=pltpu.VMEM((2, 32, 1024), F32),
    sin_t=pltpu.VMEM((2, 32, 1024), F32),
    bias=pltpu.VMEM((2, 128, 1024), F32),
    inv1=pltpu.VMEM((256, 1), F32),
    gain1=pltpu.VMEM((1, D), F32),
    gain2=pltpu.VMEM((1, D), F32),
    n1=pltpu.VMEM((2, D, 1024), BF16),
    q=pltpu.VMEM((3, 2, 128, 256), BF16),
    k=pltpu.VMEM((2, 3, 64, 1024), BF16),
    v=pltpu.VMEM((2, 3, 64, 1024), BF16),
    attn=pltpu.VMEM((2, 3, 384, 1024), BF16),
    inv_sum=pltpu.VMEM((2, 3, 384, 1), F32),
    mixed=pltpu.VMEM((2, 128, D), BF16),
    mixed_spread=pltpu.VMEM((256, DP_ROWS), BF16),
    middle=pltpu.VMEM((256, D), F32),
    inv2=pltpu.VMEM((256, 1), F32),
    n2=pltpu.VMEM((2, 256, D), BF16),
    dy=pltpu.VMEM((2, 256, D), BF16),
    dn2=pltpu.VMEM((512, D), F32),
    ahead=pltpu.VMEM((512, D), F32),
    dn2_out=pltpu.VMEM((256, D), BF16),
    dn2_in=pltpu.VMEM((256, D), BF16),
    ahead_out=pltpu.VMEM((256, D), BF16),
    ahead_in=pltpu.VMEM((256, D), BF16),
    d_middle=pltpu.VMEM((256, D), F32),
    d_mixed=pltpu.VMEM((2, 128, D), BF16),
    grad=pltpu.VMEM((D, 128), F32),
    dq=pltpu.VMEM((256, 192), F32),
    dq_pre=pltpu.VMEM((3, 256, 256), BF16),
    dn1=pltpu.VMEM((256, D), F32),
    dkv=pltpu.VMEM((3, 8, 2, 128, 128), BF16),
    dkv_in=pltpu.VMEM((3, 3, 2, 128, 128), BF16),
    relay=pltpu.VMEM((3, 3, 2, 128, 128), BF16),
    relay_sum=pltpu.VMEM((2, 128, 128), F32),
    cross=pltpu.VMEM((3, 2, 128, 128), BF16),
    cross_in=pltpu.VMEM((3, 2, 128, 128), BF16),
    dkv_sum=pltpu.VMEM((3, 2, 128, 128), F32),
    g=pltpu.VMEM((3, 4, 4, PAD, D), BF16),
    ra=pltpu.VMEM((3, 6, 2, PAD, D), BF16),
    rp=pltpu.VMEM((3, 2, 2, PAD, D), BF16),
    s2=pltpu.VMEM((3, 4, PAD, D), BF16),
    rb=pltpu.VMEM((3, 3, PAD, D), BF16),
    u=pltpu.VMEM((3, 4, 16, D), BF16),
    rc=pltpu.VMEM((3, 3, 16, D), BF16),
    f=pltpu.VMEM((PAD, D), F32),
    sum_out=split_buffers(),
    sums=[sum_buffers(384) for _ in range(3)],
)


def hand_over(*refs):
    count = len(refs) // 2
    for a, b in zip(refs[:count], refs[count:]):
        b[...] = a[...]


def local(
    inputs, segment_ids, norm_attn, w_query, w_key, w_value, w_out, norm_mlp, w_gate, w_up, w_down, cotangent,
):
    half = HEAD_WIDTH // 2
    freq = np.float32(ROPE_BASE) ** (-(np.float32(2.0) * np.arange(half, dtype=np.float32)) / HEAD_WIDTH)
    freq = freq.astype(np.float32)
    lane_freq = jnp.asarray(np.tile(freq, 4)[None, :])
    row_freq = jnp.asarray(np.tile(freq[:, None], (1, 128)))
    shapes = [
        ((2, D, 128), BF16),
        ((2, D, 128), BF16),
        ((1, ROWS), F32),
        ((ROWS, 576), F32),
        ((ROWS, 192), F32),
        ((ROWS, 192), F32),
        ((ROWS, D), F32),
        ((1, ROWS), F32),
        ((12, D), F32),
        ((12, D), F32),
        ((12, D), F32),
    ]
    shapes = [jax.ShapeDtypeStruct(shape, dtype) for shape, dtype in shapes]
    count = len(shapes)
    outs = pl.pallas_call(
        kernel,
        out_shape=shapes,
        in_specs=[pl.BlockSpec(memory_space=pl.ANY)] * 2 + [pl.BlockSpec(memory_space=pltpu.VMEM)] * 12,
        out_specs=[pl.BlockSpec(memory_space=pl.ANY)] * 2 + [pl.BlockSpec(memory_space=pltpu.VMEM)] * (count - 2),
        scratch_shapes=[SCRATCH],
        compiler_params=pltpu.CompilerParams(
            collective_id=0, has_side_effects=True, vmem_limit_bytes=60 * 2**20
        ),
        name="layer",
    )(
        jnp.transpose(inputs, (0, 2, 1)), jnp.transpose(cotangent, (0, 2, 1)), segment_ids, norm_attn[None, :],
        w_query, w_key, w_value, w_out, norm_mlp[None, :], w_gate.T, w_up.T, w_down, lane_freq, row_freq,
    )
    outs = pl.pallas_call(
        hand_over,
        out_shape=shapes,
        in_specs=[pl.BlockSpec(memory_space=pltpu.VMEM)] * count,
        out_specs=[pl.BlockSpec(memory_space=pltpu.VMEM)] * count,
        name="hand_over",
    )(*outs)
    outs = list(outs)
    for k in (0, 1):
        outs[k] = jnp.transpose(outs[k], (0, 2, 1))
    for k in (2, 7):
        outs[k] = outs[k].reshape(ROWS)
    for k in (8, 9):
        outs[k] = outs[k].T
    return tuple(outs)


def solution(mesh):
    rows, both = P("dp", None), ("dp", "seq")
    tokens = P("dp", "seq", None)
    weights = (P("dp"), rows, rows, rows, rows, P("dp"), P(None, both), P(None, both), P(both, None))
    return jax.shard_map(
        local,
        mesh=mesh,
        in_specs=(tokens, P("dp", None), *weights, tokens),
        out_specs=(tokens, tokens, *weights),
        check_vma=False,
    )
```
